32 devices in a mesh: wide: 16 (over z, y, x), narrow: 2 (over core).
Axes of the slice: x: 2, y: 2, z: 4, core: 2. Of those that a mesh axis runs over, the one named last changes fastest.
Arguments:
- point_feats: bfloat16 [8192, 512], P(('wide', 'narrow')), may hold values from -24 to 24
- region_ids: int32 [2048], P(('wide', 'narrow')), may hold values from 0 to 63, as said below
- w_qkv: bfloat16 [512, 1536], replicated, may hold values from -0.25 to 0.25
- w_out: bfloat16 [512, 512], replicated, may hold values from -0.25 to 0.25
- w_expert_in: bfloat16 [512, 131072], P(None, 'wide'), may hold values from -0.25 to 0.25
- b_expert_in: float32 [131072], P('wide'), may hold values from -4 to 4
- w_expert_out: bfloat16 [131072, 512], P('wide'), may hold values from -0.125 to 0.125
- out_cotangent: bfloat16 [8192, 512], P(('wide', 'narrow')), may hold values from -18 to 18
Outputs:
- layer_out: bfloat16 [8192, 512], P(('wide', 'narrow'))
- grad_feats: bfloat16 [8192, 512], P(('wide', 'narrow'))
- grad_attention: float32 [512, 2048], P(('wide', 'narrow'))
- grad_expert_in: float32 [512, 131072], P('narrow', 'wide')
- grad_expert_out: float32 [131072, 512], P('wide', 'narrow')
- grad_expert_bias: float32 [131072], P(('wide', 'narrow'))
The draws below stay inside these ranges and needn't reach their ends.
Inputs may be any that keep to these rules, and one draw needn't show every extreme that they name: `region_ids`: the 64 blocks of one device name any one region at most 2 times, and one region is named exactly 2 times by the blocks of every device.
All inputs are finite; a program needn't handle non-finite values.
Results may differ from the reference program's by a relative error of at most 0.0095.
Values may be sent and summed in bfloat16 or wider, within the bound.
A program may use at most 128 MiB of HBM per device.

```python
import jax
import jax.numpy as jnp
from jax import lax

D = 512
HEADS = 8
HID = 2048
DOMAIN_SPECIALS = 64
P_DEV = 256
BLOCK = 4
DOMAIN_REPEAT_CAP = 2
BPD = 64
POINTS = 8192
BLOCKS = 2048
GROUP = 2048


def shaped_field(key, low_amp, high_amp):
    noise_key, dir_key = jax.random.split(key, 2)
    devices_count = POINTS // P_DEV
    noise = jnp.clip(jax.random.normal(noise_key, (POINTS, D), jnp.float32), -6.0, 6.0)
    directions = jnp.clip(jax.random.normal(dir_key, (devices_count, D), jnp.float32), -4.0, 4.0)
    place = jnp.arange(POINTS, dtype=jnp.float32) / (POINTS - 1)
    amplitude = low_amp + (high_amp - low_amp) * place
    return noise + amplitude[:, None] * jnp.repeat(directions, P_DEV, axis=0)


def draw_point_feats(key, part):
    return shaped_field(jax.random.fold_in(key, 11), 0.6, 3.0).astype(jnp.bfloat16)


def draw_out_cotangent(key, part):
    return shaped_field(jax.random.fold_in(key, 23), 0.5, 1.5).astype(jnp.bfloat16)


def draw_region_ids(key, part):
    devices_count = BLOCKS // BPD
    hot_key, rank_key, rest_key = jax.random.split(jax.random.fold_in(key, 37), 3)
    hot_region = jax.random.randint(hot_key, (), 0, DOMAIN_SPECIALS)
    domain_frequency = jax.random.permutation(rank_key, DOMAIN_SPECIALS - 1)
    eligible_domains = jnp.arange(DOMAIN_REPEAT_CAP * (DOMAIN_SPECIALS - 1), dtype=jnp.int32) // DOMAIN_REPEAT_CAP
    others = eligible_domains + (eligible_domains >= hot_region).astype(jnp.int32)
    rating_increment = (DOMAIN_SPECIALS - 1 - domain_frequency[eligible_domains]) * 64

    def one_device(device_key):
        rating_noise_seed, order_key = jax.random.split(device_key)
        domain_ratings = jax.random.randint(rating_noise_seed, (DOMAIN_REPEAT_CAP * (DOMAIN_SPECIALS - 1),), 0, 4096) + rating_increment
        distinct = domain_ratings * (DOMAIN_REPEAT_CAP * DOMAIN_SPECIALS) + jnp.arange(DOMAIN_REPEAT_CAP * (DOMAIN_SPECIALS - 1), dtype=jnp.int32)
        chosen = lax.top_k(distinct, BPD - DOMAIN_REPEAT_CAP)[1]
        labels = jnp.concatenate([jnp.full((DOMAIN_REPEAT_CAP,), hot_region, jnp.int32), others[chosen]])
        order = jax.random.permutation(order_key, BPD)
        return labels[order]
    device_keys = jax.random.split(rest_key, devices_count)
    return jax.vmap(one_device)(device_keys).reshape(BLOCKS).astype(jnp.int32)


def shard_levels(rng, extent, cuts, low, high):
    level = 1.0
    for position, blocks in cuts:
        steps = jax.random.uniform(jax.random.fold_in(jax.random.fold_in(rng, 6), position), (blocks,), jnp.float32, low / len(cuts), high / len(cuts))
        level = level * jnp.repeat(jnp.exp(steps), extent[position] // blocks).reshape((-1,) + (1,) * (len(extent) - 1 - position))
    return level


def gaussian(key, dims, deviation, most, shards=(), kind=jnp.bfloat16):
    result = deviation * jax.random.normal(key, dims, jnp.float32)
    if shards:
        result = result * shard_levels(key, dims, shards, -0.22, 0.18)
    return jnp.clip(result, -most, most).astype(kind)


def setup_inputs(seed: int = 0) -> dict:
    seeds = jax.random.split(jax.random.key(seed), 9)
    point_feats = draw_point_feats(jax.random.fold_in(seeds[8], 71), 0)
    region_ids = draw_region_ids(jax.random.fold_in(seeds[8], 71), 0)
    w_qkv = gaussian(seeds[2], (D, 3 * D), D ** -0.5, 0.25)
    w_out = gaussian(seeds[3], (D, D), D ** -0.5, 0.25)
    w_expert_in = gaussian(seeds[4], (D, DOMAIN_SPECIALS * HID), D ** -0.5, 0.25, ((1, 16),))
    b_expert_in = gaussian(seeds[5], (DOMAIN_SPECIALS * HID,), 1.0, 4.0, ((0, 16),), jnp.float32)
    w_expert_out = gaussian(seeds[6], (DOMAIN_SPECIALS * HID, D), HID ** -0.5, 0.125, ((0, 16),))
    out_cotangent = draw_out_cotangent(jax.random.fold_in(seeds[8], 71), 0)
    return dict(point_feats=point_feats, region_ids=region_ids, w_qkv=w_qkv, w_out=w_out, w_expert_in=w_expert_in, b_expert_in=b_expert_in, w_expert_out=w_expert_out, out_cotangent=out_cotangent)


gelu_scale = 0.7978845608
gelu_cubic = 0.044715

def gelu_value(values):
    inner = gelu_scale * (values + gelu_cubic * values * values * values)
    return 0.5 * values * (1.0 + jnp.tanh(inner))

def gelu_slope(values):
    tangent = jnp.tanh(gelu_scale * (values + gelu_cubic * values * values * values))
    return 0.5 * (1.0 + tangent) + 0.5 * values * (1.0 - tangent * tangent) * gelu_scale * (1.0 + 3.0 * gelu_cubic * values * values)

def normalize_heads(raw):
    floats = raw.astype(jnp.float32)
    centred = floats - lax.optimization_barrier(jnp.mean(floats, axis=-1, keepdims=True))
    scale_dev = jnp.sqrt(lax.optimization_barrier(jnp.mean(centred * centred, axis=-1, keepdims=True)) + 1e-05)
    normed = centred / scale_dev
    return (normed.astype(jnp.bfloat16), normed, scale_dev)

def normalize_back(grad_normed, normed, scale_dev):
    mean_grad = lax.optimization_barrier(jnp.mean(grad_normed, axis=-1, keepdims=True))
    mean_cross = lax.optimization_barrier(jnp.mean(grad_normed * normed, axis=-1, keepdims=True))
    return (grad_normed - mean_grad - normed * mean_cross) / scale_dev

def round_trip(values):
    return lax.optimization_barrier(values.astype(jnp.bfloat16)).astype(jnp.float32)

def reference(point_feats, region_ids, w_qkv, w_out, w_expert_in, b_expert_in, w_expert_out, out_cotangent):
    head_dim = D // HEADS
    qkv = jnp.dot(point_feats, w_qkv, preferred_element_type=jnp.float32).astype(jnp.bfloat16)
    queries = qkv[:, :D].reshape(POINTS, HEADS, head_dim)
    key_norm, key_unit, key_scale = normalize_heads(qkv[:, D:2 * D].reshape(POINTS, HEADS, head_dim))
    value_norm, value_unit, value_scale = normalize_heads(qkv[:, 2 * D:].reshape(POINTS, HEADS, head_dim))
    summary = jnp.einsum('phi,phj->hij', key_norm.astype(jnp.float32), value_norm.astype(jnp.float32)) / POINTS
    summary_b = summary.astype(jnp.bfloat16)
    mixed = jnp.einsum('phi,hij->phj', queries.astype(jnp.float32), summary_b.astype(jnp.float32)).astype(jnp.bfloat16).reshape(POINTS, D)
    attention = jnp.dot(mixed, w_out, preferred_element_type=jnp.float32)
    grad_mixed = jnp.dot(out_cotangent, w_out.T, preferred_element_type=jnp.float32).astype(jnp.bfloat16)
    grad_heads = grad_mixed.reshape(POINTS, HEADS, head_dim)
    grad_summary = jnp.einsum('phi,phj->hij', queries.astype(jnp.float32), grad_heads.astype(jnp.float32)) / POINTS
    grad_query = jnp.einsum('phj,hij->phi', grad_heads.astype(jnp.float32), summary_b.astype(jnp.float32)).astype(jnp.bfloat16)
    grad_keynorm = jnp.einsum('phj,hij->phi', value_norm.astype(jnp.float32), grad_summary)
    grad_valnorm = jnp.einsum('phi,hij->phj', key_norm.astype(jnp.float32), grad_summary)
    grad_key = normalize_back(grad_keynorm, key_unit, key_scale).astype(jnp.bfloat16)
    grad_value = normalize_back(grad_valnorm, value_unit, value_scale).astype(jnp.bfloat16)
    grad_qkv = jnp.concatenate([grad_query.reshape(POINTS, D), grad_key.reshape(POINTS, D), grad_value.reshape(POINTS, D)], axis=1)
    attention_back = jnp.dot(grad_qkv, w_qkv.T, preferred_element_type=jnp.float32)
    grad_attention = jnp.concatenate([jnp.dot(point_feats.T, grad_qkv, preferred_element_type=jnp.float32), jnp.dot(mixed.T, out_cotangent, preferred_element_type=jnp.float32)], axis=1) / POINTS
    capacity = DOMAIN_REPEAT_CAP * (BLOCKS // BPD)
    feat_blocks = jnp.concatenate([point_feats.reshape(BLOCKS, BLOCK * D), jnp.zeros((1, BLOCK * D), jnp.bfloat16)], axis=0)
    cot_blocks = jnp.concatenate([out_cotangent.reshape(BLOCKS, BLOCK * D), jnp.zeros((1, BLOCK * D), jnp.bfloat16)], axis=0)

    def expert_step(carry, expert):
        out_acc, back_acc = carry
        members = jnp.nonzero(region_ids == expert, size=capacity, fill_value=BLOCKS)[0].astype(jnp.int32)
        rows = feat_blocks[members].reshape(capacity * BLOCK, D)
        cots = cot_blocks[members].reshape(capacity * BLOCK, D)
        live = jnp.repeat(members < BLOCKS, BLOCK)[:, None]
        w_first = lax.dynamic_slice_in_dim(w_expert_in, expert * HID, HID, 1)
        bias = lax.dynamic_slice_in_dim(b_expert_in, expert * HID, HID, 0)
        w_second = lax.dynamic_slice_in_dim(w_expert_out, expert * HID, HID, 0)
        pre_act = jnp.dot(rows, w_first, preferred_element_type=jnp.float32) + bias
        hidden = jnp.where(live, gelu_value(pre_act), 0.0).astype(jnp.bfloat16)
        grad_hidden = jnp.dot(cots, w_second.T, preferred_element_type=jnp.float32)
        grad_pre = jnp.where(live, grad_hidden * gelu_slope(pre_act), 0.0).astype(jnp.bfloat16)
        out_sum = jnp.zeros((capacity * BLOCK, D), jnp.float32)
        back_sum = jnp.zeros((capacity * BLOCK, D), jnp.float32)
        for part_index in range(HID // GROUP):
            lower = part_index * GROUP
            upper = lower + GROUP
            out_sum = out_sum + round_trip(jnp.dot(hidden[:, lower:upper], w_second[lower:upper], preferred_element_type=jnp.float32))
            back_sum = back_sum + round_trip(jnp.dot(grad_pre[:, lower:upper], w_first[:, lower:upper].T, preferred_element_type=jnp.float32))
        out_acc = out_acc.at[members].add(out_sum.reshape(capacity, BLOCK * D))
        back_acc = back_acc.at[members].add(back_sum.reshape(capacity, BLOCK * D))
        grad_second = jnp.dot(hidden.T, cots, preferred_element_type=jnp.float32)
        grad_first = jnp.dot(rows.T, grad_pre, preferred_element_type=jnp.float32)
        grad_bias = lax.optimization_barrier(jnp.sum(grad_pre.astype(jnp.float32), axis=0))
        return ((out_acc, back_acc), (grad_first, grad_second, grad_bias))
    start = (jnp.zeros((BLOCKS + 1, BLOCK * D), jnp.float32), jnp.zeros((BLOCKS + 1, BLOCK * D), jnp.float32))
    (out_acc, back_acc), (firsts, seconds, biases) = lax.scan(expert_step, start, jnp.arange(DOMAIN_SPECIALS, dtype=jnp.int32))
    expert_out = out_acc[:BLOCKS].reshape(POINTS, D)
    expert_back = back_acc[:BLOCKS].reshape(POINTS, D)
    layer_out = (point_feats.astype(jnp.float32) + attention + expert_out).astype(jnp.bfloat16)
    grad_feats = (out_cotangent.astype(jnp.float32) + attention_back + expert_back).astype(jnp.bfloat16)
    share = DOMAIN_SPECIALS / POINTS
    grad_expert_in = jnp.transpose(firsts, (1, 0, 2)).reshape(D, DOMAIN_SPECIALS * HID) * share
    grad_expert_out = seconds.reshape(DOMAIN_SPECIALS * HID, D) * share
    grad_expert_bias = biases.reshape(DOMAIN_SPECIALS * HID) * share
    return (layer_out, grad_feats, grad_attention, grad_expert_in, grad_expert_out, grad_expert_bias)
```

```python
import functools

import jax
import jax.numpy as jnp
from jax import lax
from jax.experimental import pallas as pl
from jax.experimental.pallas import tpu as pltpu
from jax.sharding import PartitionSpec as P

HEADS = 8
HID = 2048
DOMAIN_SPECIALS = 64
DOMAIN_REPEAT_CAP = 2

gelu_scale = 0.7978845608
gelu_cubic = 0.044715

F32 = jnp.float32
BF16 = jnp.bfloat16
VMEM_SPEC = pl.BlockSpec(memory_space=pltpu.VMEM)


def dot(a, b, ca=1, cb=0):
    return lax.dot_general(a, b, (((ca,), (cb,)), ((), ())), preferred_element_type=F32)


def dot_split(a, b):
    high = a.astype(BF16)
    low = (a - high.astype(F32)).astype(BF16)
    return dot(high, b) + dot(low, b)


def head_mask(width, head_dim):
    rows = lax.broadcasted_iota(jnp.int32, (width, width), 0) // head_dim
    cols = lax.broadcasted_iota(jnp.int32, (width, width), 1) // head_dim
    return rows == cols


def params(flops, size, vmem=48):
    return dict(
        cost_estimate=pl.CostEstimate(flops=flops, bytes_accessed=size, transcendentals=0),
        compiler_params=pltpu.CompilerParams(vmem_limit_bytes=vmem * 2**20),
    )


def pack_kernel(block_len, owner_count, experts_here, col_ref, row_ref, x_ref, cot_ref, pick_ref, out_ref):
    rows, points = pick_ref.shape
    width = x_ref.shape[1]
    slot_rows = experts_here * DOMAIN_REPEAT_CAP * block_len
    col, row = col_ref[...], row_ref[...]
    first = lax.broadcasted_iota(jnp.int32, (points, points), 0)
    second = lax.broadcasted_iota(jnp.int32, (points, points), 1)
    earlier = (col == row) & (first // block_len < second // block_len) & (first % block_len == 0)
    rank = jnp.sum(earlier.astype(jnp.int32), axis=0, keepdims=True)
    slot = lax.broadcasted_iota(jnp.int32, (rows, 1), 0)
    dest = slot // slot_rows
    inner = slot % slot_rows
    expert = inner // (DOMAIN_REPEAT_CAP * block_len)
    region = (dest // owner_count) * experts_here + expert
    place = (inner // block_len) % DOMAIN_REPEAT_CAP
    lane = lax.broadcasted_iota(jnp.int32, (1, points), 1) % block_len
    want = (region * DOMAIN_REPEAT_CAP + place) * block_len + slot % block_len
    have = (row * DOMAIN_REPEAT_CAP + rank) * block_len + lane
    pick = jnp.where(want == have, 1.0, 0.0).astype(BF16)
    pick_ref[...] = pick
    out_ref[:, :width] = dot(pick, x_ref[...]).astype(BF16)
    out_ref[:, width:] = dot(pick, cot_ref[...]).astype(BF16)


def first_kernel(
    total, x_ref, wqkv_ref, wout_ref, cot_ref,
    q_ref, kn_ref, vn_ref, ku_ref, vu_ref, ks_ref, vs_ref, gm_ref, sums_ref,
):
    width = x_ref.shape[1]
    head_dim = width // HEADS
    mask = head_mask(width, head_dim)
    mean_mat = jnp.where(mask, 1.0 / head_dim, 0.0).astype(BF16)

    def normalize(raw):
        centred = raw.astype(F32) - dot(raw, mean_mat)
        scale = jnp.sqrt(dot_split(centred * centred, mean_mat) + 1e-05)
        return centred / scale, scale

    def fold(full):
        kept = jnp.where(mask, full, 0.0) * (1.0 / total)
        return jnp.sum(kept.reshape(HEADS, head_dim, width), axis=0)

    x = x_ref[...]
    q = dot(x, wqkv_ref[:, :width]).astype(BF16)
    k_unit, k_scale = normalize(dot(x, wqkv_ref[:, width : 2 * width]).astype(BF16))
    v_unit, v_scale = normalize(dot(x, wqkv_ref[:, 2 * width :]).astype(BF16))
    grad_mixed = dot(cot_ref[...], wout_ref[...], 1, 1).astype(BF16)
    k_norm, v_norm = k_unit.astype(BF16), v_unit.astype(BF16)
    both = jnp.concatenate([fold(dot(k_norm, v_norm, 0, 0)), fold(dot(q, grad_mixed, 0, 0))], axis=0)
    tall = both.shape[0]
    for piece in range(width // 128):
        sums_ref[piece * tall : (piece + 1) * tall, :] = both[:, piece * 128 : (piece + 1) * 128]
    q_ref[...] = q
    kn_ref[...] = k_norm
    vn_ref[...] = v_norm
    ku_ref[...] = k_unit
    vu_ref[...] = v_unit
    ks_ref[...] = k_scale
    vs_ref[...] = v_scale
    gm_ref[...] = grad_mixed


def second_kernel(
    total, sums_ref, x_ref, wqkv_ref, wout_ref, cot_ref,
    q_ref, kn_ref, vn_ref, ku_ref, vu_ref, ks_ref, vs_ref, gm_ref,
    att_ref, out_ref, back_ref,
):
    width = x_ref.shape[1]
    head_dim = width // HEADS
    mask = head_mask(width, head_dim)
    mean_mat = jnp.where(mask, 1.0 / head_dim, 0.0).astype(BF16)
    tall = sums_ref.shape[0] // (width // 128)
    both = jnp.concatenate([sums_ref[p * tall : (p + 1) * tall, :] for p in range(width // 128)], axis=1)

    def spread(folded):
        whole = jnp.concatenate([folded] * HEADS, axis=0)
        return jnp.where(mask, whole, 0.0).astype(BF16)

    summary = spread(both[:head_dim])
    grad_summary = spread(both[head_dim:])

    def back(grad, unit, scale):
        mean_grad = dot_split(grad, mean_mat)
        mean_cross = dot_split(grad * unit, mean_mat)
        return ((grad - mean_grad - unit * mean_cross) / scale).astype(BF16)

    x, cot = x_ref[...], cot_ref[...]
    mixed = dot(q_ref[...], summary).astype(BF16)
    grad_query = dot(gm_ref[...], summary, 1, 1).astype(BF16)
    grad_key = back(dot(vn_ref[...], grad_summary, 1, 1), ku_ref[...], ks_ref[...])
    grad_value = back(dot(kn_ref[...], grad_summary), vu_ref[...], vs_ref[...])
    scale = 1.0 / total
    x_turned = x.T
    att_ref[:, :width] = (dot(x_turned, grad_query) * scale).astype(BF16)
    att_ref[:, width : 2 * width] = (dot(x_turned, grad_key) * scale).astype(BF16)
    att_ref[:, 2 * width : 3 * width] = (dot(x_turned, grad_value) * scale).astype(BF16)
    att_ref[:, 3 * width :] = (dot(mixed, cot, 0, 0) * scale).astype(BF16)
    out_ref[...] = x.astype(F32) + dot(mixed, wout_ref[...])
    back_ref[...] = (
        cot.astype(F32)
        + dot(grad_query, wqkv_ref[:, :width], 1, 1)
        + dot(grad_key, wqkv_ref[:, width : 2 * width], 1, 1)
        + dot(grad_value, wqkv_ref[:, 2 * width :], 1, 1)
    )


def expert_kernel(
    share, half_ref, feat_ref, cot_ref, feat_half_ref, cot_half_ref, win_ref, bias_ref, wout_ref,
    ret_ref, gin_ref, gout_ref, gbias_ref, out_acc, back_acc,
):
    step = pl.program_id(1)
    own, width = out_acc.shape
    w_in, w_out = win_ref[...], wout_ref[...]
    pre = dot(feat_ref[0], w_in) + bias_ref[...]
    grad_hidden = dot(cot_ref[0], w_out, 1, 1)
    square = pre * pre
    tangent = jnp.tanh(gelu_scale * (pre + gelu_cubic * square * pre))
    half_sum = 0.5 * (1.0 + tangent)
    hidden = (pre * half_sum).astype(BF16)
    slope = half_sum + 0.5 * pre * (1.0 - tangent * tangent) * gelu_scale * (1.0 + 3.0 * gelu_cubic * square)
    grad_pre = (grad_hidden * slope).astype(BF16)
    out_part = dot(hidden[:own], w_out)
    back_part = dot(grad_pre[:own], w_in, 1, 1)

    @pl.when(step == 0)
    def _():
        out_acc[...] = out_part
        back_acc[...] = back_part

    @pl.when(step > 0)
    def _():
        out_acc[...] += out_part
        back_acc[...] += back_part

    gin_ref[...] = dot(feat_half_ref[0], grad_pre, 0, 0) * share
    gout_ref[...] = dot(hidden, cot_half_ref[0], 0, 0) * share
    gbias_ref[...] = jnp.sum(grad_pre.astype(F32), axis=0, keepdims=True) * share

    @pl.when(step == pl.num_programs(1) - 1)
    def _():
        ret_ref[0, :, :width] = out_acc[...].astype(BF16)
        ret_ref[0, :, width:] = back_acc[...].astype(BF16)


def final_kernel(pick_ref, ret_ref, out_base_ref, back_base_ref, out_ref, back_ref):
    width = out_ref.shape[1]
    picked = dot(pick_ref[...], ret_ref[...], 0, 0)
    out_ref[...] = (out_base_ref[...] + picked[:, :width]).astype(BF16)
    back_ref[...] = (back_base_ref[...] + picked[:, width:]).astype(BF16)


def on_device(
    point_feats, region_ids, w_qkv, w_out, w_expert_in, b_expert_in, w_expert_out, out_cotangent
):
    wide_count = lax.axis_size("wide")
    narrow_count = lax.axis_size("narrow")
    device_count = wide_count * narrow_count
    narrow_index = lax.axis_index("narrow")
    swap = [(i, (i + 1) % narrow_count) for i in range(narrow_count)]
    points, width = point_feats.shape
    total = points * device_count
    blocks = region_ids.shape[0]
    block_len = points // blocks
    slab = w_expert_in.shape[1]
    owner_count = max(1, wide_count // DOMAIN_SPECIALS)
    experts_here = max(1, DOMAIN_SPECIALS // wide_count)
    hid_here = slab // experts_here
    slot_rows = DOMAIN_REPEAT_CAP * block_len
    rows = wide_count * experts_here * slot_rows
    own = rows // experts_here

    labels = jnp.repeat(region_ids, block_len)
    pick, packed = pl.pallas_call(
        functools.partial(pack_kernel, block_len, owner_count, experts_here),
        out_shape=(
            jax.ShapeDtypeStruct((rows, points), BF16),
            jax.ShapeDtypeStruct((rows, 2 * width), BF16),
        ),
        in_specs=[VMEM_SPEC] * 4,
        out_specs=[VMEM_SPEC] * 2,
        name="pack",
        **params(4 * rows * points * width, 4 * rows * width),
    )(labels[:, None], labels[None, :], point_feats, out_cotangent)
    received = lax.all_to_all(packed, "wide", split_axis=0, concat_axis=0, tiled=True)

    wide_bf = jax.ShapeDtypeStruct((points, width), BF16)
    wide_f = jax.ShapeDtypeStruct((points, width), F32)
    fold_rows = 2 * (width // HEADS) * (width // 128)
    *kept, sums = pl.pallas_call(
        functools.partial(first_kernel, total),
        out_shape=(
            wide_bf, wide_bf, wide_bf, wide_f, wide_f, wide_f, wide_f, wide_bf,
            jax.ShapeDtypeStruct((fold_rows, 128), F32),
        ),
        in_specs=[VMEM_SPEC] * 4,
        out_specs=[VMEM_SPEC] * 9,
        name="first",
        **params(20 * points * width * width, 8 * points * width),
    )(point_feats, w_qkv, w_out, out_cotangent)
    axes = ("wide", "narrow")
    pieces = lax.all_to_all(sums, axes, split_axis=0, concat_axis=0, tiled=True)
    piece = jnp.sum(pieces.reshape(device_count, fold_rows // device_count, 128), axis=0)
    copies = jnp.broadcast_to(piece[None], (device_count,) + piece.shape).reshape(fold_rows, 128)
    sums = lax.all_to_all(copies, axes, split_axis=0, concat_axis=0, tiled=True)
    att, out_base, back_base = pl.pallas_call(
        functools.partial(second_kernel, total),
        out_shape=(jax.ShapeDtypeStruct((width, 4 * width), BF16), wide_f, wide_f),
        in_specs=[VMEM_SPEC] * 13,
        out_specs=[VMEM_SPEC] * 3,
        name="second",
        **params(30 * points * width * width, 8 * points * width),
    )(sums, point_feats, w_qkv, w_out, out_cotangent, *kept)
    att = att.reshape(wide_count, narrow_count, width // device_count, 4 * width)
    mine = lax.dynamic_index_in_dim(att, narrow_index, 1, keepdims=False)
    for shift in range(1, narrow_count):
        other = lax.rem(narrow_index + shift, narrow_count)
        theirs = lax.dynamic_index_in_dim(att, other, 1, keepdims=False)
        perm = [(i, (i + shift) % narrow_count) for i in range(narrow_count)]
        mine = mine.astype(F32) + lax.ppermute(theirs, "narrow", perm).astype(F32)
    mine = mine.astype(BF16).reshape(wide_count * (width // device_count), 4 * width)
    att_parts = lax.all_to_all(mine, "wide", split_axis=0, concat_axis=0, tiled=True)
    grad_attention = jnp.sum(
        att_parts.reshape(wide_count, width // device_count, 4 * width).astype(F32), axis=0
    )

    parts = [received]
    for shift in range(1, narrow_count):
        perm = [(i, (i + shift) % narrow_count) for i in range(narrow_count)]
        parts.append(lax.ppermute(received, "narrow", perm))
    by_expert = [
        part.reshape(wide_count, experts_here, slot_rows, 2 * width)
        .transpose(1, 0, 2, 3)
        .reshape(experts_here, own, 2 * width)
        for part in parts
    ]
    gathered = jnp.concatenate(by_expert, axis=1)
    all_rows = own * narrow_count
    tile = min(512, hid_here)
    steps = hid_here // tile
    half = width // narrow_count
    share = DOMAIN_SPECIALS / total
    returned, grad_in, grad_out_w, grad_bias = pl.pallas_call(
        functools.partial(expert_kernel, share),
        out_shape=(
            jax.ShapeDtypeStruct((experts_here, own, 2 * width), BF16),
            jax.ShapeDtypeStruct((half, slab), F32),
            jax.ShapeDtypeStruct((slab, half), F32),
            jax.ShapeDtypeStruct((1, slab), F32),
        ),
        grid_spec=pltpu.PrefetchScalarGridSpec(
            num_scalar_prefetch=1,
            grid=(experts_here, steps),
            in_specs=[
                pl.BlockSpec((1, all_rows, width), lambda e, t, n: (e, 0, 0)),
                pl.BlockSpec((1, all_rows, width), lambda e, t, n: (e, 0, 1)),
                pl.BlockSpec((1, all_rows, half), lambda e, t, n: (e, 0, n[0])),
                pl.BlockSpec((1, all_rows, half), lambda e, t, n: (e, 0, narrow_count + n[0])),
                pl.BlockSpec((width, tile), lambda e, t, n: (0, e * steps + t)),
                pl.BlockSpec((1, tile), lambda e, t, n: (0, e * steps + t)),
                pl.BlockSpec((tile, width), lambda e, t, n: (e * steps + t, 0)),
            ],
            out_specs=[
                pl.BlockSpec((1, own, 2 * width), lambda e, t, n: (e, 0, 0)),
                pl.BlockSpec((half, tile), lambda e, t, n: (0, e * steps + t)),
                pl.BlockSpec((tile, half), lambda e, t, n: (e * steps + t, 0)),
                pl.BlockSpec((1, tile), lambda e, t, n: (0, e * steps + t)),
            ],
            scratch_shapes=[pltpu.VMEM((own, width), F32), pltpu.VMEM((own, width), F32)],
        ),
        name="experts",
        **params(8 * all_rows * width * slab, 8 * width * slab),
    )(
        narrow_index.astype(jnp.int32)[None],
        gathered, gathered, gathered, gathered,
        w_expert_in, b_expert_in[None, :], w_expert_out,
    )
    returned = (
        returned.reshape(experts_here, wide_count, slot_rows, 2 * width)
        .transpose(1, 0, 2, 3)
        .reshape(rows, 2 * width)
    )
    returned = lax.all_to_all(returned, "wide", split_axis=0, concat_axis=0, tiled=True)
    layer_out, grad_feats = pl.pallas_call(
        final_kernel,
        out_shape=(wide_bf, wide_bf),
        in_specs=[VMEM_SPEC] * 4,
        out_specs=[VMEM_SPEC] * 2,
        name="final",
        **params(4 * rows * points * width, 4 * rows * width),
    )(pick, returned, out_base, back_base)
    bias_half = slab // narrow_count
    grad_bias_out = lax.dynamic_slice_in_dim(grad_bias[0], narrow_index * bias_half, bias_half, 0)
    return (layer_out, grad_feats, grad_attention, grad_in, grad_out_w, grad_bias_out)


def solution(mesh):
    placed = (
        P(("wide", "narrow"), None),
        P(("wide", "narrow")),
        P(),
        P(),
        P(None, "wide"),
        P("wide"),
        P("wide", None),
        P(("wide", "narrow"), None),
    )
    return jax.shard_map(
        on_device,
        mesh=mesh,
        in_specs=placed,
        out_specs=(
            P(("wide", "narrow"), None),
            P(("wide", "narrow"), None),
            P(("wide", "narrow"), None),
            P("narrow", "wide"),
            P("wide", "narrow"),
            P(("wide", "narrow")),
        ),
        check_vma=False,
    )
```

```python
import functools

import jax
import jax.numpy as jnp
from jax import lax
from jax.experimental import pallas as pl
from jax.experimental.pallas import tpu as pltpu
from jax.sharding import PartitionSpec as P

HEADS = 8
HID = 2048
DOMAIN_SPECIALS = 64
DOMAIN_REPEAT_CAP = 2

gelu_scale = 0.7978845608
gelu_cubic = 0.044715

F32 = jnp.float32
BF16 = jnp.bfloat16
VMEM_SPEC = pl.BlockSpec(memory_space=pltpu.VMEM)


def dot(a, b, ca=1, cb=0):
    return lax.dot_general(a, b, (((ca,), (cb,)), ((), ())), preferred_element_type=F32)


def dot_split(a, b):
    high = a.astype(BF16)
    low = (a - high.astype(F32)).astype(BF16)
    return dot(high, b) + dot(low, b)


def head_mask(width, head_dim):
    rows = lax.broadcasted_iota(jnp.int32, (width, width), 0) // head_dim
    cols = lax.broadcasted_iota(jnp.int32, (width, width), 1) // head_dim
    return rows == cols


def params(flops, size, vmem=48):
    return dict(
        cost_estimate=pl.CostEstimate(flops=flops, bytes_accessed=size, transcendentals=0),
        compiler_params=pltpu.CompilerParams(vmem_limit_bytes=vmem * 2**20),
    )


def pack_kernel(block_len, owner_count, experts_here, col_ref, row_ref, x_ref, cot_ref, pick_ref, out_ref):
    rows, points = pick_ref.shape
    width = x_ref.shape[1]
    slot_rows = experts_here * DOMAIN_REPEAT_CAP * block_len
    col, row = col_ref[...], row_ref[...]
    first = lax.broadcasted_iota(jnp.int32, (points, points), 0)
    second = lax.broadcasted_iota(jnp.int32, (points, points), 1)
    earlier = (col == row) & (first // block_len < second // block_len) & (first % block_len == 0)
    rank = jnp.sum(earlier.astype(jnp.int32), axis=0, keepdims=True)
    slot = lax.broadcasted_iota(jnp.int32, (rows, 1), 0)
    dest = slot // slot_rows
    inner = slot % slot_rows
    expert = inner // (DOMAIN_REPEAT_CAP * block_len)
    region = (dest // owner_count) * experts_here + expert
    place = (inner // block_len) % DOMAIN_REPEAT_CAP
    lane = lax.broadcasted_iota(jnp.int32, (1, points), 1) % block_len
    want = (region * DOMAIN_REPEAT_CAP + place) * block_len + slot % block_len
    have = (row * DOMAIN_REPEAT_CAP + rank) * block_len + lane
    pick = jnp.where(want == have, 1.0, 0.0).astype(BF16)
    pick_ref[...] = pick
    out_ref[:, :width] = dot(pick, x_ref[...]).astype(BF16)
    out_ref[:, width:] = dot(pick, cot_ref[...]).astype(BF16)


def first_kernel(
    total, x_ref, wqkv_ref, wout_ref, cot_ref,
    q_ref, kn_ref, vn_ref, ku_ref, vu_ref, ks_ref, vs_ref, gm_ref, sums_ref,
):
    width = x_ref.shape[1]
    head_dim = width // HEADS
    mask = head_mask(width, head_dim)
    mean_mat = jnp.where(mask, 1.0 / head_dim, 0.0).astype(BF16)

    def normalize(raw):
        centred = raw.astype(F32) - dot(raw, mean_mat)
        scale = jnp.sqrt(dot_split(centred * centred, mean_mat) + 1e-05)
        return centred / scale, scale

    def fold(full):
        kept = jnp.where(mask, full, 0.0) * (1.0 / total)
        return jnp.sum(kept.reshape(HEADS, head_dim, width), axis=0)

    x = x_ref[...]
    q = dot(x, wqkv_ref[:, :width]).astype(BF16)
    k_unit, k_scale = normalize(dot(x, wqkv_ref[:, width : 2 * width]).astype(BF16))
    v_unit, v_scale = normalize(dot(x, wqkv_ref[:, 2 * width :]).astype(BF16))
    grad_mixed = dot(cot_ref[...], wout_ref[...], 1, 1).astype(BF16)
    k_norm, v_norm = k_unit.astype(BF16), v_unit.astype(BF16)
    both = jnp.concatenate([fold(dot(k_norm, v_norm, 0, 0)), fold(dot(q, grad_mixed, 0, 0))], axis=0)
    tall = both.shape[0]
    for piece in range(width // 128):
        sums_ref[piece * tall : (piece + 1) * tall, :] = both[:, piece * 128 : (piece + 1) * 128]
    q_ref[...] = q
    kn_ref[...] = k_norm
    vn_ref[...] = v_norm
    ku_ref[...] = k_unit
    vu_ref[...] = v_unit
    ks_ref[...] = k_scale
    vs_ref[...] = v_scale
    gm_ref[...] = grad_mixed


def second_kernel(
    total, sums_ref, x_ref, wqkv_ref, wout_ref, cot_ref,
    q_ref, kn_ref, vn_ref, ku_ref, vu_ref, ks_ref, vs_ref, gm_ref,
    att_ref, out_ref, back_ref,
):
    width = x_ref.shape[1]
    head_dim = width // HEADS
    mask = head_mask(width, head_dim)
    mean_mat = jnp.where(mask, 1.0 / head_dim, 0.0).astype(BF16)
    tall = sums_ref.shape[0] // (width // 128)
    both = jnp.concatenate([sums_ref[p * tall : (p + 1) * tall, :] for p in range(width // 128)], axis=1)

    def spread(folded):
        whole = jnp.concatenate([folded] * HEADS, axis=0)
        return jnp.where(mask, whole, 0.0).astype(BF16)

    summary = spread(both[:head_dim])
    grad_summary = spread(both[head_dim:])

    def back(grad, unit, scale):
        mean_grad = dot_split(grad, mean_mat)
        mean_cross = dot_split(grad * unit, mean_mat)
        return ((grad - mean_grad - unit * mean_cross) / scale).astype(BF16)

    x, cot = x_ref[...], cot_ref[...]
    mixed = dot(q_ref[...], summary).astype(BF16)
    grad_query = dot(gm_ref[...], summary, 1, 1).astype(BF16)
    grad_key = back(dot(vn_ref[...], grad_summary, 1, 1), ku_ref[...], ks_ref[...])
    grad_value = back(dot(kn_ref[...], grad_summary), vu_ref[...], vs_ref[...])
    scale = 1.0 / total
    x_turned = x.T
    att_ref[:, :width] = (dot(x_turned, grad_query) * scale).astype(BF16)
    att_ref[:, width : 2 * width] = (dot(x_turned, grad_key) * scale).astype(BF16)
    att_ref[:, 2 * width : 3 * width] = (dot(x_turned, grad_value) * scale).astype(BF16)
    att_ref[:, 3 * width :] = (dot(mixed, cot, 0, 0) * scale).astype(BF16)
    out_ref[...] = x.astype(F32) + dot(mixed, wout_ref[...])
    back_ref[...] = (
        cot.astype(F32)
        + dot(grad_query, wqkv_ref[:, :width], 1, 1)
        + dot(grad_key, wqkv_ref[:, width : 2 * width], 1, 1)
        + dot(grad_value, wqkv_ref[:, 2 * width :], 1, 1)
    )


def expert_kernel(
    share, half_ref, feat_ref, cot_ref, feat_half_ref, cot_half_ref, win_ref, bias_ref, wout_ref,
    ret_ref, gin_ref, gout_ref, gbias_ref, out_acc, back_acc,
):
    step = pl.program_id(1)
    own, width = out_acc.shape
    w_in, w_out = win_ref[...], wout_ref[...]
    pre = dot(feat_ref[0], w_in) + bias_ref[...]
    grad_hidden = dot(cot_ref[0], w_out, 1, 1)
    square = pre * pre
    tangent = jnp.tanh(gelu_scale * (pre + gelu_cubic * square * pre))
    half_sum = 0.5 * (1.0 + tangent)
    hidden = (pre * half_sum).astype(BF16)
    slope = half_sum + 0.5 * pre * (1.0 - tangent * tangent) * gelu_scale * (1.0 + 3.0 * gelu_cubic * square)
    grad_pre = (grad_hidden * slope).astype(BF16)
    out_part = dot(hidden[:own], w_out)
    back_part = dot(grad_pre[:own], w_in, 1, 1)

    @pl.when(step == 0)
    def _():
        out_acc[...] = out_part
        back_acc[...] = back_part

    @pl.when(step > 0)
    def _():
        out_acc[...] += out_part
        back_acc[...] += back_part

    gin_ref[...] = dot(feat_half_ref[0], grad_pre, 0, 0) * share
    gout_ref[...] = dot(hidden, cot_half_ref[0], 0, 0) * share
    gbias_ref[...] = jnp.sum(grad_pre.astype(F32), axis=0, keepdims=True) * share

    @pl.when(step == pl.num_programs(1) - 1)
    def _():
        ret_ref[0, :, :width] = out_acc[...].astype(BF16)
        ret_ref[0, :, width:] = back_acc[...].astype(BF16)


def final_kernel(pick_ref, ret_ref, out_base_ref, back_base_ref, out_ref, back_ref):
    width = out_ref.shape[1]
    picked = dot(pick_ref[...], ret_ref[...], 0, 0)
    out_ref[...] = (out_base_ref[...] + picked[:, :width]).astype(BF16)
    back_ref[...] = (back_base_ref[...] + picked[:, width:]).astype(BF16)


def on_device_plain(
    point_feats, region_ids, w_qkv, w_out, w_expert_in, b_expert_in, w_expert_out, out_cotangent
):
    wide_count = lax.axis_size("wide")
    narrow_count = lax.axis_size("narrow")
    device_count = wide_count * narrow_count
    narrow_index = lax.axis_index("narrow")
    swap = [(i, (i + 1) % narrow_count) for i in range(narrow_count)]
    points, width = point_feats.shape
    total = points * device_count
    blocks = region_ids.shape[0]
    block_len = points // blocks
    slab = w_expert_in.shape[1]
    owner_count = max(1, wide_count // DOMAIN_SPECIALS)
    experts_here = max(1, DOMAIN_SPECIALS // wide_count)
    hid_here = slab // experts_here
    slot_rows = DOMAIN_REPEAT_CAP * block_len
    rows = wide_count * experts_here * slot_rows
    own = rows // experts_here

    labels = jnp.repeat(region_ids, block_len)
    pick, packed = pl.pallas_call(
        functools.partial(pack_kernel, block_len, owner_count, experts_here),
        out_shape=(
            jax.ShapeDtypeStruct((rows, points), BF16),
            jax.ShapeDtypeStruct((rows, 2 * width), BF16),
        ),
        in_specs=[VMEM_SPEC] * 4,
        out_specs=[VMEM_SPEC] * 2,
        name="pack",
        **params(4 * rows * points * width, 4 * rows * width),
    )(labels[:, None], labels[None, :], point_feats, out_cotangent)
    received = lax.all_to_all(packed, "wide", split_axis=0, concat_axis=0, tiled=True)

    wide_bf = jax.ShapeDtypeStruct((points, width), BF16)
    wide_f = jax.ShapeDtypeStruct((points, width), F32)
    fold_rows = 2 * (width // HEADS) * (width // 128)
    *kept, sums = pl.pallas_call(
        functools.partial(first_kernel, total),
        out_shape=(
            wide_bf, wide_bf, wide_bf, wide_f, wide_f, wide_f, wide_f, wide_bf,
            jax.ShapeDtypeStruct((fold_rows, 128), F32),
        ),
        in_specs=[VMEM_SPEC] * 4,
        out_specs=[VMEM_SPEC] * 9,
        name="first",
        **params(20 * points * width * width, 8 * points * width),
    )(point_feats, w_qkv, w_out, out_cotangent)
    axes = ("wide", "narrow")
    pieces = lax.all_to_all(sums, axes, split_axis=0, concat_axis=0, tiled=True)
    piece = jnp.sum(pieces.reshape(device_count, fold_rows // device_count, 128), axis=0)
    copies = jnp.broadcast_to(piece[None], (device_count,) + piece.shape).reshape(fold_rows, 128)
    sums = lax.all_to_all(copies, axes, split_axis=0, concat_axis=0, tiled=True)
    att, out_base, back_base = pl.pallas_call(
        functools.partial(second_kernel, total),
        out_shape=(jax.ShapeDtypeStruct((width, 4 * width), BF16), wide_f, wide_f),
        in_specs=[VMEM_SPEC] * 13,
        out_specs=[VMEM_SPEC] * 3,
        name="second",
        **params(30 * points * width * width, 8 * points * width),
    )(sums, point_feats, w_qkv, w_out, out_cotangent, *kept)
    att = att.reshape(wide_count, narrow_count, width // device_count, 4 * width)
    mine = lax.dynamic_index_in_dim(att, narrow_index, 1, keepdims=False)
    for shift in range(1, narrow_count):
        other = lax.rem(narrow_index + shift, narrow_count)
        theirs = lax.dynamic_index_in_dim(att, other, 1, keepdims=False)
        perm = [(i, (i + shift) % narrow_count) for i in range(narrow_count)]
        mine = mine.astype(F32) + lax.ppermute(theirs, "narrow", perm).astype(F32)
    mine = mine.astype(BF16).reshape(wide_count * (width // device_count), 4 * width)
    att_parts = lax.all_to_all(mine, "wide", split_axis=0, concat_axis=0, tiled=True)
    grad_attention = jnp.sum(
        att_parts.reshape(wide_count, width // device_count, 4 * width).astype(F32), axis=0
    )

    parts = [received]
    for shift in range(1, narrow_count):
        perm = [(i, (i + shift) % narrow_count) for i in range(narrow_count)]
        parts.append(lax.ppermute(received, "narrow", perm))
    by_expert = [
        part.reshape(wide_count, experts_here, slot_rows, 2 * width)
        .transpose(1, 0, 2, 3)
        .reshape(experts_here, own, 2 * width)
        for part in parts
    ]
    gathered = jnp.concatenate(by_expert, axis=1)
    all_rows = own * narrow_count
    tile = min(512, hid_here)
    steps = hid_here // tile
    half = width // narrow_count
    share = DOMAIN_SPECIALS / total
    returned, grad_in, grad_out_w, grad_bias = pl.pallas_call(
        functools.partial(expert_kernel, share),
        out_shape=(
            jax.ShapeDtypeStruct((experts_here, own, 2 * width), BF16),
            jax.ShapeDtypeStruct((half, slab), F32),
            jax.ShapeDtypeStruct((slab, half), F32),
            jax.ShapeDtypeStruct((1, slab), F32),
        ),
        grid_spec=pltpu.PrefetchScalarGridSpec(
            num_scalar_prefetch=1,
            grid=(experts_here, steps),
            in_specs=[
                pl.BlockSpec((1, all_rows, width), lambda e, t, n: (e, 0, 0)),
                pl.BlockSpec((1, all_rows, width), lambda e, t, n: (e, 0, 1)),
                pl.BlockSpec((1, all_rows, half), lambda e, t, n: (e, 0, n[0])),
                pl.BlockSpec((1, all_rows, half), lambda e, t, n: (e, 0, narrow_count + n[0])),
                pl.BlockSpec((width, tile), lambda e, t, n: (0, e * steps + t)),
                pl.BlockSpec((1, tile), lambda e, t, n: (0, e * steps + t)),
                pl.BlockSpec((tile, width), lambda e, t, n: (e * steps + t, 0)),
            ],
            out_specs=[
                pl.BlockSpec((1, own, 2 * width), lambda e, t, n: (e, 0, 0)),
                pl.BlockSpec((half, tile), lambda e, t, n: (0, e * steps + t)),
                pl.BlockSpec((tile, half), lambda e, t, n: (e * steps + t, 0)),
                pl.BlockSpec((1, tile), lambda e, t, n: (0, e * steps + t)),
            ],
            scratch_shapes=[pltpu.VMEM((own, width), F32), pltpu.VMEM((own, width), F32)],
        ),
        name="experts",
        **params(8 * all_rows * width * slab, 8 * width * slab),
    )(
        narrow_index.astype(jnp.int32)[None],
        gathered, gathered, gathered, gathered,
        w_expert_in, b_expert_in[None, :], w_expert_out,
    )
    returned = (
        returned.reshape(experts_here, wide_count, slot_rows, 2 * width)
        .transpose(1, 0, 2, 3)
        .reshape(rows, 2 * width)
    )
    returned = lax.all_to_all(returned, "wide", split_axis=0, concat_axis=0, tiled=True)
    layer_out, grad_feats = pl.pallas_call(
        final_kernel,
        out_shape=(wide_bf, wide_bf),
        in_specs=[VMEM_SPEC] * 4,
        out_specs=[VMEM_SPEC] * 2,
        name="final",
        **params(4 * rows * points * width, 4 * rows * width),
    )(pick, returned, out_base, back_base)
    bias_half = slab // narrow_count
    grad_bias_out = lax.dynamic_slice_in_dim(grad_bias[0], narrow_index * bias_half, bias_half, 0)
    return (layer_out, grad_feats, grad_attention, grad_in, grad_out_w, grad_bias_out)


MESH = pl.DeviceIdType.MESH


def slot_have(block_len, col, row):
    points = row.shape[1]
    first = lax.broadcasted_iota(jnp.int32, (points, points), 0)
    second = lax.broadcasted_iota(jnp.int32, (points, points), 1)
    earlier = (col == row) & (first // block_len < second // block_len) & (first % block_len == 0)
    rank = jnp.sum(earlier.astype(jnp.int32), axis=0, keepdims=True)
    lane = lax.broadcasted_iota(jnp.int32, (1, points), 1) % block_len
    return (row * DOMAIN_REPEAT_CAP + rank) * block_len + lane


def slot_picks(block_len, experts, expert, rows, have):
    slot_rows = DOMAIN_REPEAT_CAP * block_len
    slot = lax.broadcasted_iota(jnp.int32, (rows, 1), 0)
    region = (slot // (2 * slot_rows)) * experts + expert
    second = (slot // slot_rows) % 2
    place = (slot % slot_rows) // block_len
    want = (region * DOMAIN_REPEAT_CAP + place) * block_len + slot % block_len
    low = jnp.where(second == 0, want, -1)
    high = jnp.where(second == 1, want, -1)
    return [jnp.where(side == have, 1.0, 0.0).astype(BF16) for side in (low, high)]


def remote(src, dst, send, recv, device):
    return pltpu.make_async_remote_copy(
        src_ref=src, dst_ref=dst, send_sem=send, recv_sem=recv, device_id=device, device_id_type=MESH
    )


def attend_kernel(
    dims, col_ref, row_ref, x_ref, cot_ref, wqkv_ref, wout_ref,
    gath_ref, mine_ref, out_ref, back_ref,
    packed, sums, parts, piece, totals, att, theirs,
    s_one, r_one, s_two, r_two, s_send, r_send, s_pair, r_pair, s_half, r_half,
):
    wide, narrow, experts, block_len, total = dims
    devices = wide * narrow
    chunk = 2 * DOMAIN_REPEAT_CAP * block_len
    here, side = lax.axis_index("wide"), lax.axis_index("narrow")
    me = here * narrow + side
    partner = (here, 1 - side)
    width = x_ref.shape[1]
    head_dim = width // HEADS

    def peer(k):
        index = (me + k) % devices
        return index, (index // narrow, index % narrow)

    barrier = pltpu.get_barrier_semaphore()

    def greet(k, carry):
        pl.semaphore_signal(barrier, inc=1, device_id=peer(k)[1], device_id_type=MESH)
        return carry

    lax.fori_loop(1, devices, greet, 0)

    mask = head_mask(width, head_dim)
    mean_mat = jnp.where(mask, 1.0 / head_dim, 0.0).astype(BF16)

    def normalize(raw):
        centred = raw.astype(F32) - dot(raw, mean_mat)
        scale = jnp.sqrt(dot_split(centred * centred, mean_mat) + 1e-05)
        return centred / scale, scale

    def fold(full):
        kept = jnp.where(mask, full, 0.0) * (1.0 / total)
        return jnp.sum(kept.reshape(HEADS, head_dim, width), axis=0)

    x, cot = x_ref[...], cot_ref[...]
    q = dot(x, wqkv_ref[:, :width]).astype(BF16)
    k_unit, k_scale = normalize(dot(x, wqkv_ref[:, width : 2 * width]).astype(BF16))
    v_unit, v_scale = normalize(dot(x, wqkv_ref[:, 2 * width :]).astype(BF16))
    grad_mixed = dot(cot, wout_ref[...], 1, 1).astype(BF16)
    k_norm, v_norm = k_unit.astype(BF16), v_unit.astype(BF16)
    both = jnp.concatenate([fold(dot(k_norm, v_norm, 0, 0)), fold(dot(q, grad_mixed, 0, 0))], axis=0)
    tall = jnp.concatenate([both[:, p * 128 : (p + 1) * 128] for p in range(width // 128)], axis=0)
    sums[...] = tall.reshape(sums.shape)
    pl.semaphore_wait(barrier, devices - 1)

    def one(k):
        index, device = peer(k)
        return remote(sums.at[index], parts.at[k], s_one.at[k], r_one.at[k], device)

    def two(k):
        return remote(piece, totals.at[me], s_two.at[k], r_two.at[k], peer(k)[1])

    def span(index):
        return pl.ds(pl.multiple_of(index * chunk, chunk), chunk)

    def send(k):
        dest = (here + k) % wide
        return remote(
            packed.at[span(dest)], gath_ref.at[span(here)], s_send.at[k], r_send.at[k], (dest, side)
        )

    def forward(k):
        source = (here - k + wide) % wide
        return remote(
            gath_ref.at[span(source)], gath_ref.at[span(wide + source)],
            s_pair.at[k], r_pair.at[k], partner,
        )

    def each(low, high, action):
        def body(k, carry):
            action(k)
            return carry

        lax.fori_loop(low, high, body, 0)

    each(1, devices, lambda k: one(k).start())
    parts[0] = sums[me]
    have = slot_have(block_len, col_ref[...], row_ref[...])
    for expert in range(experts):
        first, second = slot_picks(block_len, experts, expert, packed.shape[0], have)
        packed[:, expert * width : (expert + 1) * width] = (dot(first, x) + dot(second, cot)).astype(BF16)
    each(1, devices, lambda k: one(k).wait_recv())
    whole = jnp.sum(parts[...], axis=0)
    piece[...] = whole
    totals[me] = whole
    each(1, devices, lambda k: two(k).start())
    each(1, wide, lambda k: send(k).start())
    gath_ref[span(here), :] = packed[span(here), :]
    forward(0).start()
    each(1, devices, lambda k: two(k).wait_recv())

    tall = totals[...].reshape(devices * totals.shape[1], 128)
    step = tall.shape[0] // (width // 128)
    both = jnp.concatenate([tall[p * step : (p + 1) * step] for p in range(width // 128)], axis=1)

    def spread(folded):
        return jnp.where(mask, jnp.concatenate([folded] * HEADS, axis=0), 0.0).astype(BF16)

    summary, grad_summary = spread(both[:head_dim]), spread(both[head_dim:])

    def back(grad, unit, scale):
        mean_grad = dot_split(grad, mean_mat)
        mean_cross = dot_split(grad * unit, mean_mat)
        return ((grad - mean_grad - unit * mean_cross) / scale).astype(BF16)

    mixed = dot(q, summary).astype(BF16)
    grad_query = dot(grad_mixed, summary, 1, 1).astype(BF16)
    grad_key = back(dot(v_norm, grad_summary, 1, 1), k_unit, k_scale)
    grad_value = back(dot(k_norm, grad_summary), v_unit, v_scale)
    x_turned = x.T
    mixed_turned = mixed.T
    for block, (left, right) in enumerate(
        [(x_turned, grad_query), (x_turned, grad_key), (x_turned, grad_value), (mixed_turned, cot)]
    ):
        value = (dot(left, right) * (1.0 / total)).reshape(wide, narrow, -1, width)
        for part in range(narrow):
            att[part, :, :, block * width : (block + 1) * width] = value[:, part].astype(BF16)
    swap = remote(att.at[1 - side], theirs, s_half, r_half, partner)
    swap.start()
    out_ref[...] = x.astype(F32) + dot(mixed, wout_ref[...])
    back_ref[...] = (
        cot.astype(F32)
        + dot(grad_query, wqkv_ref[:, :width], 1, 1)
        + dot(grad_key, wqkv_ref[:, width : 2 * width], 1, 1)
        + dot(grad_value, wqkv_ref[:, 2 * width :], 1, 1)
    )
    swap.wait()
    mine_ref[...] = (att[side].astype(F32) + theirs[...].astype(F32)).astype(BF16)

    def pass_on(k):
        send(k).wait_recv()
        forward(k).start()

    each(1, wide, pass_on)
    each(0, wide, lambda k: forward(k).wait_recv())
    each(0, wide, lambda k: forward(k).wait_send())
    each(1, wide, lambda k: send(k).wait_send())
    each(1, devices, lambda k: one(k).wait_send())
    each(1, devices, lambda k: two(k).wait_send())


def split_rows(block, slot_rows):
    rows, width = block.shape
    floats = block.astype(F32).reshape(rows // (2 * slot_rows), 2, slot_rows, width)
    return [floats[:, i].reshape(rows // 2, width).astype(BF16) for i in range(2)]


def region_kernel(
    dims, gath_ref, win_ref, bias_ref, wout_ref, mine_ref, col_ref, row_ref, out_base_ref, back_base_ref,
    hidden_ref, gpre_ref, out_ref, back_ref, gatt_ref,
    feats, cots, out_acc, back_acc, ret_send, ret_recv, stage_one, stage_sum, stage_two,
    s_ret, r_ret, s_one, r_one, s_two, r_two,
):
    wide, plane, experts, block_len = dims
    levels = wide // plane
    slot_rows = DOMAIN_REPEAT_CAP * block_len
    chunk = 2 * slot_rows
    here, side = lax.axis_index("wide"), lax.axis_index("narrow")
    level, spot = here // plane, here % plane
    expert, step = pl.program_id(0), pl.program_id(1)
    last_step = pl.num_programs(1) - 1
    own, width = out_acc.shape

    def each(low, high, action):
        def body(k, carry):
            action(k)
            return carry

        lax.fori_loop(low, high, body, 0)

    def span(index):
        return pl.ds(pl.multiple_of(index * chunk, chunk), chunk)

    def give(e, k):
        dest = (here + k) % wide
        return remote(
            ret_send.at[e, span(dest)], ret_recv.at[e, span(here)],
            s_ret.at[e, k], r_ret.at[e, k], (dest, side),
        )

    def one(k):
        other = (spot + k) % plane
        return remote(
            mine_ref.at[:, other], stage_one.at[k], s_one.at[k], r_one.at[k],
            (level * plane + other, side),
        )

    def two(k):
        other = (level + k) % levels
        return remote(
            stage_sum.at[other], stage_two.at[k], s_two.at[k], r_two.at[k],
            (other * plane + spot, side),
        )

    @pl.when((expert == 0) & (step == 0))
    def _():
        barrier = pltpu.get_barrier_semaphore()
        each(
            1, wide,
            lambda k: pl.semaphore_signal(
                barrier, inc=1, device_id=((here + k) % wide, side), device_id_type=MESH
            ),
        )
        pl.semaphore_wait(barrier, wide - 1)
        each(1, plane, lambda k: one(k).start())
        stage_one[0] = mine_ref[:, spot]

    @pl.when((expert == 1) & (step == 0))
    def _():
        each(1, plane, lambda k: one(k).wait())
        summed = jnp.sum(stage_one[...].astype(F32), axis=0).astype(BF16)
        stage_sum[...] = summed
        each(1, levels, lambda k: two(k).start())
        stage_two[0] = stage_sum[level]

    @pl.when(step == 0)
    def _():
        feats[...], cots[...] = split_rows(gath_ref[...], slot_rows)

    w_in, w_out = win_ref[...], wout_ref[...]
    pre = dot(feats[...], w_in) + bias_ref[...]
    grad_hidden = dot(cots[...], w_out, 1, 1)
    square = pre * pre
    tangent = jnp.tanh(gelu_scale * (pre + gelu_cubic * square * pre))
    half_sum = 0.5 * (1.0 + tangent)
    hidden = (pre * half_sum).astype(BF16)
    slope = half_sum + 0.5 * pre * (1.0 - tangent * tangent) * gelu_scale * (1.0 + 3.0 * gelu_cubic * square)
    grad_pre = (grad_hidden * slope).astype(BF16)
    hidden_ref[...] = hidden
    gpre_ref[...] = grad_pre
    out_part = dot(hidden[:own], w_out)
    back_part = dot(grad_pre[:own], w_in, 1, 1)

    @pl.when(step == 0)
    def _():
        out_acc[...] = out_part
        back_acc[...] = back_part

    @pl.when(step > 0)
    def _():
        out_acc[...] += out_part
        back_acc[...] += back_part

    @pl.when(step == last_step)
    def _():
        pair = jnp.concatenate(
            [ref[...].reshape(wide, slot_rows, width) for ref in (out_acc, back_acc)], axis=1
        )
        ret_send[expert] = pair.reshape(wide * chunk, width).astype(BF16)
        each(1, wide, lambda k: give(expert, k).start())
        ret_recv[expert, span(here), :] = ret_send[expert, span(here), :]

    @pl.when((expert == experts - 1) & (step == last_step))
    def _():
        each(1, levels, lambda k: two(k).wait())
        gatt_ref[...] = jnp.sum(stage_two[...].astype(F32), axis=0)
        have = slot_have(block_len, col_ref[...], row_ref[...])
        out, back = out_base_ref[...], back_base_ref[...]
        for e in range(experts):
            each(1, wide, lambda k: give(e, k).wait_recv())
            first, second = slot_picks(block_len, experts, e, wide * chunk, have)
            rows = ret_recv[e]
            out += dot(first, rows, 0, 0)
            back += dot(second, rows, 0, 0)
        out_ref[...] = out.astype(BF16)
        back_ref[...] = back.astype(BF16)
        for e in range(experts):
            each(1, wide, lambda k: give(e, k).wait_send())


def weight_kernel(
    share, slot_rows, half_ref, gath_feat_ref, hidden_ref, gpre_ref, gin_ref, gout_ref, gbias_ref, feats, cots
):
    @pl.when(pl.program_id(1) == 0)
    def _():
        feat, cot = split_rows(gath_feat_ref[...], slot_rows)
        feats[...] = feat.T
        cots[...] = cot

    grad_pre = gpre_ref[...]
    gin_ref[...] = dot(feats[...], grad_pre) * share
    gout_ref[...] = dot(hidden_ref[...], cots[...], 0, 0) * share
    gbias_ref[...] = jnp.sum(grad_pre.astype(F32), axis=0, keepdims=True) * share


def on_device(
    point_feats, region_ids, w_qkv, w_out, w_expert_in, b_expert_in, w_expert_out, out_cotangent
):
    wide = lax.axis_size("wide")
    narrow = lax.axis_size("narrow")
    devices = wide * narrow
    points, width = point_feats.shape
    total = points * devices
    block_len = points // region_ids.shape[0]
    slab = w_expert_in.shape[1]
    experts = DOMAIN_SPECIALS // wide
    plane = 4
    if narrow != 2 or experts < 2 or wide % plane or width % (16 * devices):
        return on_device_plain(
            point_feats, region_ids, w_qkv, w_out, w_expert_in, b_expert_in, w_expert_out, out_cotangent
        )
    hid = slab // experts
    slot_rows = DOMAIN_REPEAT_CAP * block_len
    chunk = 2 * slot_rows
    fold_rows = 2 * (width // HEADS) * (width // 128) // devices
    share_rows = width // devices
    labels = jnp.repeat(region_ids, block_len)
    col, row = labels[:, None], labels[None, :]
    wide_bf = jax.ShapeDtypeStruct((points, width), BF16)
    wide_f = jax.ShapeDtypeStruct((points, width), F32)
    dma = pltpu.SemaphoreType.DMA

    def remote_params(identity):
        return pltpu.CompilerParams(
            collective_id=identity, has_side_effects=True, vmem_limit_bytes=48 * 2**20
        )

    gathered, mine, out_base, back_base = pl.pallas_call(
        functools.partial(attend_kernel, (wide, narrow, experts, block_len, total)),
        out_shape=(
            jax.ShapeDtypeStruct((narrow * wide * chunk, experts * width), BF16),
            jax.ShapeDtypeStruct((wide, share_rows, 4 * width), BF16),
            wide_f, wide_f,
        ),
        in_specs=[VMEM_SPEC] * 6,
        out_specs=[VMEM_SPEC] * 4,
        scratch_shapes=[
            pltpu.VMEM((wide * chunk, experts * width), BF16),
            pltpu.VMEM((devices, fold_rows, 128), F32),
            pltpu.VMEM((devices, fold_rows, 128), F32),
            pltpu.VMEM((fold_rows, 128), F32),
            pltpu.VMEM((devices, fold_rows, 128), F32),
            pltpu.VMEM((narrow, wide, share_rows, 4 * width), BF16),
            pltpu.VMEM((wide, share_rows, 4 * width), BF16),
            dma((devices,)), dma((devices,)), dma((devices,)), dma((devices,)),
            dma((wide,)), dma((wide,)), dma((wide,)), dma((wide,)), dma, dma,
        ],
        compiler_params=remote_params(0),
        name="attend",
    )(col, row, point_feats, out_cotangent, w_qkv, w_out)

    own = wide * slot_rows
    all_rows = own * narrow
    tile = min(512, hid)
    steps = hid // tile
    levels = wide // plane
    slab_bf = jax.ShapeDtypeStruct((all_rows, slab), BF16)
    hidden, grad_pre, layer_out, grad_feats, grad_attention = pl.pallas_call(
        functools.partial(region_kernel, (wide, plane, experts, block_len)),
        out_shape=(
            slab_bf, slab_bf, wide_bf, wide_bf, jax.ShapeDtypeStruct((share_rows, 4 * width), F32),
        ),
        grid=(experts, steps),
        in_specs=[
            pl.BlockSpec((narrow * wide * chunk, width), lambda e, t: (0, e)),
            pl.BlockSpec((width, tile), lambda e, t: (0, e * steps + t)),
            pl.BlockSpec((1, tile), lambda e, t: (0, e * steps + t)),
            pl.BlockSpec((tile, width), lambda e, t: (e * steps + t, 0)),
        ] + [VMEM_SPEC] * 5,
        out_specs=[
            pl.BlockSpec((all_rows, tile), lambda e, t: (0, e * steps + t)),
            pl.BlockSpec((all_rows, tile), lambda e, t: (0, e * steps + t)),
        ] + [VMEM_SPEC] * 3,
        scratch_shapes=[
            pltpu.VMEM((all_rows, width), BF16),
            pltpu.VMEM((all_rows, width), BF16),
            pltpu.VMEM((own, width), F32),
            pltpu.VMEM((own, width), F32),
            pltpu.VMEM((experts, wide * chunk, width), BF16),
            pltpu.VMEM((experts, wide * chunk, width), BF16),
            pltpu.VMEM((plane, levels, share_rows, 4 * width), BF16),
            pltpu.VMEM((levels, share_rows, 4 * width), BF16),
            pltpu.VMEM((levels, share_rows, 4 * width), BF16),
            dma((experts, wide)), dma((experts, wide)),
            dma((plane,)), dma((plane,)), dma((levels,)), dma((levels,)),
        ],
        compiler_params=remote_params(1),
        name="regions",
    )(
        gathered, w_expert_in, b_expert_in[None, :], w_expert_out,
        mine.reshape(levels, plane, share_rows, 4 * width), col, row, out_base, back_base,
    )

    half = width // narrow
    side = lax.axis_index("narrow")
    wtile = min(1024, hid)
    wsteps = hid // wtile
    grad_in, grad_out_w, grad_bias = pl.pallas_call(
        functools.partial(weight_kernel, DOMAIN_SPECIALS / total, slot_rows),
        out_shape=(
            jax.ShapeDtypeStruct((half, slab), F32),
            jax.ShapeDtypeStruct((slab, half), F32),
            jax.ShapeDtypeStruct((1, slab), F32),
        ),
        grid_spec=pltpu.PrefetchScalarGridSpec(
            num_scalar_prefetch=1,
            grid=(experts, wsteps),
            in_specs=[
                pl.BlockSpec((narrow * wide * chunk, half), lambda e, t, n: (0, e * narrow + n[0])),
                pl.BlockSpec((all_rows, wtile), lambda e, t, n: (0, e * wsteps + t)),
                pl.BlockSpec((all_rows, wtile), lambda e, t, n: (0, e * wsteps + t)),
            ],
            out_specs=[
                pl.BlockSpec((half, wtile), lambda e, t, n: (0, e * wsteps + t)),
                pl.BlockSpec((wtile, half), lambda e, t, n: (e * wsteps + t, 0)),
                pl.BlockSpec((1, wtile), lambda e, t, n: (0, e * wsteps + t)),
            ],
            scratch_shapes=[pltpu.VMEM((half, all_rows), BF16), pltpu.VMEM((all_rows, half), BF16)],
        ),
        name="weights",
        **params(8 * all_rows * half * slab, 8 * width * slab),
    )(side.astype(jnp.int32)[None], gathered, hidden, grad_pre)
    bias_half = slab // narrow
    grad_bias_out = lax.dynamic_slice_in_dim(grad_bias[0], side * bias_half, bias_half, 0)
    return (layer_out, grad_feats, grad_attention, grad_in, grad_out_w, grad_bias_out)


def solution(mesh):
    placed = (
        P(("wide", "narrow"), None),
        P(("wide", "narrow")),
        P(),
        P(),
        P(None, "wide"),
        P("wide"),
        P("wide", None),
        P(("wide", "narrow"), None),
    )
    return jax.shard_map(
        on_device,
        mesh=mesh,
        in_specs=placed,
        out_specs=(
            P(("wide", "narrow"), None),
            P(("wide", "narrow"), None),
            P(("wide", "narrow"), None),
            P("narrow", "wide"),
            P("wide", "narrow"),
            P(("wide", "narrow")),
        ),
        check_vma=False,
    )
```

```python
import functools

import jax
import jax.numpy as jnp
from jax import lax
from jax.experimental import pallas as pl
from jax.experimental.pallas import tpu as pltpu
from jax.sharding import PartitionSpec as P

HEADS = 8
HID = 2048
DOMAIN_SPECIALS = 64
DOMAIN_REPEAT_CAP = 2

gelu_scale = 0.7978845608
gelu_cubic = 0.044715

F32 = jnp.float32
BF16 = jnp.bfloat16
VMEM_SPEC = pl.BlockSpec(memory_space=pltpu.VMEM)
HBM_SPEC = pl.BlockSpec(memory_space=pltpu.HBM)


def dot(a, b, ca=1, cb=0):
    return lax.dot_general(a, b, (((ca,), (cb,)), ((), ())), preferred_element_type=F32)


def dot_split(a, b):
    high = a.astype(BF16)
    low = (a - high.astype(F32)).astype(BF16)
    return dot(high, b) + dot(low, b)


def head_mask(width, head_dim):
    rows = lax.broadcasted_iota(jnp.int32, (width, width), 0) // head_dim
    cols = lax.broadcasted_iota(jnp.int32, (width, width), 1) // head_dim
    return rows == cols


def params(flops, size, vmem=48):
    return dict(
        cost_estimate=pl.CostEstimate(flops=flops, bytes_accessed=size, transcendentals=0),
        compiler_params=pltpu.CompilerParams(vmem_limit_bytes=vmem * 2**20),
    )


def pack_kernel(block_len, owner_count, experts_here, col_ref, row_ref, x_ref, cot_ref, pick_ref, out_ref):
    rows, points = pick_ref.shape
    width = x_ref.shape[1]
    slot_rows = experts_here * DOMAIN_REPEAT_CAP * block_len
    col, row = col_ref[...], row_ref[...]
    first = lax.broadcasted_iota(jnp.int32, (points, points), 0)
    second = lax.broadcasted_iota(jnp.int32, (points, points), 1)
    earlier = (col == row) & (first // block_len < second // block_len) & (first % block_len == 0)
    rank = jnp.sum(earlier.astype(jnp.int32), axis=0, keepdims=True)
    slot = lax.broadcasted_iota(jnp.int32, (rows, 1), 0)
    dest = slot // slot_rows
    inner = slot % slot_rows
    expert = inner // (DOMAIN_REPEAT_CAP * block_len)
    region = (dest // owner_count) * experts_here + expert
    place = (inner // block_len) % DOMAIN_REPEAT_CAP
    lane = lax.broadcasted_iota(jnp.int32, (1, points), 1) % block_len
    want = (region * DOMAIN_REPEAT_CAP + place) * block_len + slot % block_len
    have = (row * DOMAIN_REPEAT_CAP + rank) * block_len + lane
    pick = jnp.where(want == have, 1.0, 0.0).astype(BF16)
    pick_ref[...] = pick
    out_ref[:, :width] = dot(pick, x_ref[...]).astype(BF16)
    out_ref[:, width:] = dot(pick, cot_ref[...]).astype(BF16)


def first_kernel(
    total, x_ref, wqkv_ref, wout_ref, cot_ref,
    q_ref, kn_ref, vn_ref, ku_ref, vu_ref, ks_ref, vs_ref, gm_ref, sums_ref,
):
    width = x_ref.shape[1]
    head_dim = width // HEADS
    mask = head_mask(width, head_dim)
    mean_mat = jnp.where(mask, 1.0 / head_dim, 0.0).astype(BF16)

    def normalize(raw):
        centred = raw.astype(F32) - dot(raw, mean_mat)
        scale = jnp.sqrt(dot_split(centred * centred, mean_mat) + 1e-05)
        return centred / scale, scale

    def fold(full):
        kept = jnp.where(mask, full, 0.0) * (1.0 / total)
        return jnp.sum(kept.reshape(HEADS, head_dim, width), axis=0)

    x = x_ref[...]
    q = dot(x, wqkv_ref[:, :width]).astype(BF16)
    k_unit, k_scale = normalize(dot(x, wqkv_ref[:, width : 2 * width]).astype(BF16))
    v_unit, v_scale = normalize(dot(x, wqkv_ref[:, 2 * width :]).astype(BF16))
    grad_mixed = dot(cot_ref[...], wout_ref[...], 1, 1).astype(BF16)
    k_norm, v_norm = k_unit.astype(BF16), v_unit.astype(BF16)
    both = jnp.concatenate([fold(dot(k_norm, v_norm, 0, 0)), fold(dot(q, grad_mixed, 0, 0))], axis=0)
    tall = both.shape[0]
    for piece in range(width // 128):
        sums_ref[piece * tall : (piece + 1) * tall, :] = both[:, piece * 128 : (piece + 1) * 128]
    q_ref[...] = q
    kn_ref[...] = k_norm
    vn_ref[...] = v_norm
    ku_ref[...] = k_unit
    vu_ref[...] = v_unit
    ks_ref[...] = k_scale
    vs_ref[...] = v_scale
    gm_ref[...] = grad_mixed


def second_kernel(
    total, sums_ref, x_ref, wqkv_ref, wout_ref, cot_ref,
    q_ref, kn_ref, vn_ref, ku_ref, vu_ref, ks_ref, vs_ref, gm_ref,
    att_ref, out_ref, back_ref,
):
    width = x_ref.shape[1]
    head_dim = width // HEADS
    mask = head_mask(width, head_dim)
    mean_mat = jnp.where(mask, 1.0 / head_dim, 0.0).astype(BF16)
    tall = sums_ref.shape[0] // (width // 128)
    both = jnp.concatenate([sums_ref[p * tall : (p + 1) * tall, :] for p in range(width // 128)], axis=1)

    def spread(folded):
        whole = jnp.concatenate([folded] * HEADS, axis=0)
        return jnp.where(mask, whole, 0.0).astype(BF16)

    summary = spread(both[:head_dim])
    grad_summary = spread(both[head_dim:])

    def back(grad, unit, scale):
        mean_grad = dot_split(grad, mean_mat)
        mean_cross = dot_split(grad * unit, mean_mat)
        return ((grad - mean_grad - unit * mean_cross) / scale).astype(BF16)

    x, cot = x_ref[...], cot_ref[...]
    mixed = dot(q_ref[...], summary).astype(BF16)
    grad_query = dot(gm_ref[...], summary, 1, 1).astype(BF16)
    grad_key = back(dot(vn_ref[...], grad_summary, 1, 1), ku_ref[...], ks_ref[...])
    grad_value = back(dot(kn_ref[...], grad_summary), vu_ref[...], vs_ref[...])
    scale = 1.0 / total
    x_turned = x.T
    att_ref[:, :width] = (dot(x_turned, grad_query) * scale).astype(BF16)
    att_ref[:, width : 2 * width] = (dot(x_turned, grad_key) * scale).astype(BF16)
    att_ref[:, 2 * width : 3 * width] = (dot(x_turned, grad_value) * scale).astype(BF16)
    att_ref[:, 3 * width :] = (dot(mixed, cot, 0, 0) * scale).astype(BF16)
    out_ref[...] = x.astype(F32) + dot(mixed, wout_ref[...])
    back_ref[...] = (
        cot.astype(F32)
        + dot(grad_query, wqkv_ref[:, :width], 1, 1)
        + dot(grad_key, wqkv_ref[:, width : 2 * width], 1, 1)
        + dot(grad_value, wqkv_ref[:, 2 * width :], 1, 1)
    )


def expert_kernel(
    share, half_ref, feat_ref, cot_ref, feat_half_ref, cot_half_ref, win_ref, bias_ref, wout_ref,
    ret_ref, gin_ref, gout_ref, gbias_ref, out_acc, back_acc,
):
    step = pl.program_id(1)
    own, width = out_acc.shape
    w_in, w_out = win_ref[...], wout_ref[...]
    pre = dot(feat_ref[0], w_in) + bias_ref[...]
    grad_hidden = dot(cot_ref[0], w_out, 1, 1)
    square = pre * pre
    tangent = jnp.tanh(gelu_scale * (pre + gelu_cubic * square * pre))
    half_sum = 0.5 * (1.0 + tangent)
    hidden = (pre * half_sum).astype(BF16)
    slope = half_sum + 0.5 * pre * (1.0 - tangent * tangent) * gelu_scale * (1.0 + 3.0 * gelu_cubic * square)
    grad_pre = (grad_hidden * slope).astype(BF16)
    out_part = dot(hidden[:own], w_out)
    back_part = dot(grad_pre[:own], w_in, 1, 1)

    @pl.when(step == 0)
    def _():
        out_acc[...] = out_part
        back_acc[...] = back_part

    @pl.when(step > 0)
    def _():
        out_acc[...] += out_part
        back_acc[...] += back_part

    gin_ref[...] = dot(feat_half_ref[0], grad_pre, 0, 0) * share
    gout_ref[...] = dot(hidden, cot_half_ref[0], 0, 0) * share
    gbias_ref[...] = jnp.sum(grad_pre.astype(F32), axis=0, keepdims=True) * share

    @pl.when(step == pl.num_programs(1) - 1)
    def _():
        ret_ref[0, :, :width] = out_acc[...].astype(BF16)
        ret_ref[0, :, width:] = back_acc[...].astype(BF16)


def final_kernel(pick_ref, ret_ref, out_base_ref, back_base_ref, out_ref, back_ref):
    width = out_ref.shape[1]
    picked = dot(pick_ref[...], ret_ref[...], 0, 0)
    out_ref[...] = (out_base_ref[...] + picked[:, :width]).astype(BF16)
    back_ref[...] = (back_base_ref[...] + picked[:, width:]).astype(BF16)


def on_device_plain(
    point_feats, region_ids, w_qkv, w_out, w_expert_in, b_expert_in, w_expert_out, out_cotangent
):
    wide_count = lax.axis_size("wide")
    narrow_count = lax.axis_size("narrow")
    device_count = wide_count * narrow_count
    narrow_index = lax.axis_index("narrow")
    swap = [(i, (i + 1) % narrow_count) for i in range(narrow_count)]
    points, width = point_feats.shape
    total = points * device_count
    blocks = region_ids.shape[0]
    block_len = points // blocks
    slab = w_expert_in.shape[1]
    owner_count = max(1, wide_count // DOMAIN_SPECIALS)
    experts_here = max(1, DOMAIN_SPECIALS // wide_count)
    hid_here = slab // experts_here
    slot_rows = DOMAIN_REPEAT_CAP * block_len
    rows = wide_count * experts_here * slot_rows
    own = rows // experts_here

    labels = jnp.repeat(region_ids, block_len)
    pick, packed = pl.pallas_call(
        functools.partial(pack_kernel, block_len, owner_count, experts_here),
        out_shape=(
            jax.ShapeDtypeStruct((rows, points), BF16),
            jax.ShapeDtypeStruct((rows, 2 * width), BF16),
        ),
        in_specs=[VMEM_SPEC] * 4,
        out_specs=[VMEM_SPEC] * 2,
        name="pack",
        **params(4 * rows * points * width, 4 * rows * width),
    )(labels[:, None], labels[None, :], point_feats, out_cotangent)
    received = lax.all_to_all(packed, "wide", split_axis=0, concat_axis=0, tiled=True)

    wide_bf = jax.ShapeDtypeStruct((points, width), BF16)
    wide_f = jax.ShapeDtypeStruct((points, width), F32)
    fold_rows = 2 * (width // HEADS) * (width // 128)
    *kept, sums = pl.pallas_call(
        functools.partial(first_kernel, total),
        out_shape=(
            wide_bf, wide_bf, wide_bf, wide_f, wide_f, wide_f, wide_f, wide_bf,
            jax.ShapeDtypeStruct((fold_rows, 128), F32),
        ),
        in_specs=[VMEM_SPEC] * 4,
        out_specs=[VMEM_SPEC] * 9,
        name="first",
        **params(20 * points * width * width, 8 * points * width),
    )(point_feats, w_qkv, w_out, out_cotangent)
    axes = ("wide", "narrow")
    pieces = lax.all_to_all(sums, axes, split_axis=0, concat_axis=0, tiled=True)
    piece = jnp.sum(pieces.reshape(device_count, fold_rows // device_count, 128), axis=0)
    copies = jnp.broadcast_to(piece[None], (device_count,) + piece.shape).reshape(fold_rows, 128)
    sums = lax.all_to_all(copies, axes, split_axis=0, concat_axis=0, tiled=True)
    att, out_base, back_base = pl.pallas_call(
        functools.partial(second_kernel, total),
        out_shape=(jax.ShapeDtypeStruct((width, 4 * width), BF16), wide_f, wide_f),
        in_specs=[VMEM_SPEC] * 13,
        out_specs=[VMEM_SPEC] * 3,
        name="second",
        **params(30 * points * width * width, 8 * points * width),
    )(sums, point_feats, w_qkv, w_out, out_cotangent, *kept)
    att = att.reshape(wide_count, narrow_count, width // device_count, 4 * width)
    mine = lax.dynamic_index_in_dim(att, narrow_index, 1, keepdims=False)
    for shift in range(1, narrow_count):
        other = lax.rem(narrow_index + shift, narrow_count)
        theirs = lax.dynamic_index_in_dim(att, other, 1, keepdims=False)
        perm = [(i, (i + shift) % narrow_count) for i in range(narrow_count)]
        mine = mine.astype(F32) + lax.ppermute(theirs, "narrow", perm).astype(F32)
    mine = mine.astype(BF16).reshape(wide_count * (width // device_count), 4 * width)
    att_parts = lax.all_to_all(mine, "wide", split_axis=0, concat_axis=0, tiled=True)
    grad_attention = jnp.sum(
        att_parts.reshape(wide_count, width // device_count, 4 * width).astype(F32), axis=0
    )

    parts = [received]
    for shift in range(1, narrow_count):
        perm = [(i, (i + shift) % narrow_count) for i in range(narrow_count)]
        parts.append(lax.ppermute(received, "narrow", perm))
    by_expert = [
        part.reshape(wide_count, experts_here, slot_rows, 2 * width)
        .transpose(1, 0, 2, 3)
        .reshape(experts_here, own, 2 * width)
        for part in parts
    ]
    gathered = jnp.concatenate(by_expert, axis=1)
    all_rows = own * narrow_count
    tile = min(512, hid_here)
    steps = hid_here // tile
    half = width // narrow_count
    share = DOMAIN_SPECIALS / total
    returned, grad_in, grad_out_w, grad_bias = pl.pallas_call(
        functools.partial(expert_kernel, share),
        out_shape=(
            jax.ShapeDtypeStruct((experts_here, own, 2 * width), BF16),
            jax.ShapeDtypeStruct((half, slab), F32),
            jax.ShapeDtypeStruct((slab, half), F32),
            jax.ShapeDtypeStruct((1, slab), F32),
        ),
        grid_spec=pltpu.PrefetchScalarGridSpec(
            num_scalar_prefetch=1,
            grid=(experts_here, steps),
            in_specs=[
                pl.BlockSpec((1, all_rows, width), lambda e, t, n: (e, 0, 0)),
                pl.BlockSpec((1, all_rows, width), lambda e, t, n: (e, 0, 1)),
                pl.BlockSpec((1, all_rows, half), lambda e, t, n: (e, 0, n[0])),
                pl.BlockSpec((1, all_rows, half), lambda e, t, n: (e, 0, narrow_count + n[0])),
                pl.BlockSpec((width, tile), lambda e, t, n: (0, e * steps + t)),
                pl.BlockSpec((1, tile), lambda e, t, n: (0, e * steps + t)),
                pl.BlockSpec((tile, width), lambda e, t, n: (e * steps + t, 0)),
            ],
            out_specs=[
                pl.BlockSpec((1, own, 2 * width), lambda e, t, n: (e, 0, 0)),
                pl.BlockSpec((half, tile), lambda e, t, n: (0, e * steps + t)),
                pl.BlockSpec((tile, half), lambda e, t, n: (e * steps + t, 0)),
                pl.BlockSpec((1, tile), lambda e, t, n: (0, e * steps + t)),
            ],
            scratch_shapes=[pltpu.VMEM((own, width), F32), pltpu.VMEM((own, width), F32)],
        ),
        name="experts",
        **params(8 * all_rows * width * slab, 8 * width * slab),
    )(
        narrow_index.astype(jnp.int32)[None],
        gathered, gathered, gathered, gathered,
        w_expert_in, b_expert_in[None, :], w_expert_out,
    )
    returned = (
        returned.reshape(experts_here, wide_count, slot_rows, 2 * width)
        .transpose(1, 0, 2, 3)
        .reshape(rows, 2 * width)
    )
    returned = lax.all_to_all(returned, "wide", split_axis=0, concat_axis=0, tiled=True)
    layer_out, grad_feats = pl.pallas_call(
        final_kernel,
        out_shape=(wide_bf, wide_bf),
        in_specs=[VMEM_SPEC] * 4,
        out_specs=[VMEM_SPEC] * 2,
        name="final",
        **params(4 * rows * points * width, 4 * rows * width),
    )(pick, returned, out_base, back_base)
    bias_half = slab // narrow_count
    grad_bias_out = lax.dynamic_slice_in_dim(grad_bias[0], narrow_index * bias_half, bias_half, 0)
    return (layer_out, grad_feats, grad_attention, grad_in, grad_out_w, grad_bias_out)


MESH = pl.DeviceIdType.MESH


def slot_have(block_len, col, row):
    points = row.shape[1]
    first = lax.broadcasted_iota(jnp.int32, (points, points), 0)
    second = lax.broadcasted_iota(jnp.int32, (points, points), 1)
    earlier = (col == row) & (first // block_len < second // block_len) & (first % block_len == 0)
    rank = jnp.sum(earlier.astype(jnp.int32), axis=0, keepdims=True)
    lane = lax.broadcasted_iota(jnp.int32, (1, points), 1) % block_len
    return (row * DOMAIN_REPEAT_CAP + rank) * block_len + lane


def slot_picks(block_len, experts, expert, rows, have):
    slot_rows = DOMAIN_REPEAT_CAP * block_len
    slot = lax.broadcasted_iota(jnp.int32, (rows, 1), 0)
    region = (slot // (2 * slot_rows)) * experts + expert
    second = (slot // slot_rows) % 2
    place = (slot % slot_rows) // block_len
    want = (region * DOMAIN_REPEAT_CAP + place) * block_len + slot % block_len
    low = jnp.where(second == 0, want, -1)
    high = jnp.where(second == 1, want, -1)
    return [jnp.where(side == have, 1.0, 0.0).astype(BF16) for side in (low, high)]


def remote(src, dst, send, recv, device):
    return pltpu.make_async_remote_copy(
        src_ref=src, dst_ref=dst, send_sem=send, recv_sem=recv, device_id=device, device_id_type=MESH
    )


def attend_kernel(
    dims, col_ref, row_ref, x_hbm, cot_hbm, wqkv_hbm, wout_hbm,
    gath_ref, mine_ref, out_ref, back_ref,
    x_ref, cot_ref, wqkv_ref, wout_ref, packed, sums, parts, piece, totals, att, theirs,
    s_one, r_one, s_two, r_two, s_send, r_send, s_pair, r_pair, s_half, r_half, s_in, s_own,
):
    wide, narrow, experts, block_len, total = dims
    devices = wide * narrow
    chunk = 2 * DOMAIN_REPEAT_CAP * block_len
    here, side = lax.axis_index("wide"), lax.axis_index("narrow")
    me = here * narrow + side
    partner = (here, 1 - side)
    width = x_ref.shape[1]
    head_dim = width // HEADS

    def peer(k):
        index = (me + k) % devices
        return index, (index // narrow, index % narrow)

    sources = [(x_hbm, x_ref), (cot_hbm, cot_ref), (wqkv_hbm, wqkv_ref), (wout_hbm, wout_ref)]
    loads = [pltpu.make_async_copy(a, b, s_in.at[i]) for i, (a, b) in enumerate(sources)]
    for load in loads:
        load.start()
    barrier = pltpu.get_barrier_semaphore()

    def greet(k, carry):
        pl.semaphore_signal(barrier, inc=1, device_id=peer(k)[1], device_id_type=MESH)
        return carry

    lax.fori_loop(1, devices, greet, 0)

    mask = head_mask(width, head_dim)
    mean_mat = jnp.where(mask, 1.0 / head_dim, 0.0).astype(BF16)

    def normalize(raw):
        centred = raw.astype(F32) - dot(raw, mean_mat)
        scale = jnp.sqrt(dot_split(centred * centred, mean_mat) + 1e-05)
        return centred / scale, scale

    def fold(full):
        kept = jnp.where(mask, full, 0.0) * (1.0 / total)
        return jnp.sum(kept.reshape(HEADS, head_dim, width), axis=0)

    loads[0].wait()
    loads[1].wait()
    x, cot = x_ref[...], cot_ref[...]
    have = slot_have(block_len, col_ref[...], row_ref[...])
    for expert in range(experts):
        first, second = slot_picks(block_len, experts, expert, packed.shape[0], have)
        packed[:, expert * width : (expert + 1) * width] = (dot(first, x) + dot(second, cot)).astype(BF16)
    loads[2].wait()
    loads[3].wait()
    q = dot(x, wqkv_ref[:, :width]).astype(BF16)
    k_unit, k_scale = normalize(dot(x, wqkv_ref[:, width : 2 * width]).astype(BF16))
    v_unit, v_scale = normalize(dot(x, wqkv_ref[:, 2 * width :]).astype(BF16))
    grad_mixed = dot(cot, wout_ref[...], 1, 1).astype(BF16)
    k_norm, v_norm = k_unit.astype(BF16), v_unit.astype(BF16)
    both = jnp.concatenate([fold(dot(k_norm, v_norm, 0, 0)), fold(dot(q, grad_mixed, 0, 0))], axis=0)
    tall = jnp.concatenate([both[:, p * 128 : (p + 1) * 128] for p in range(width // 128)], axis=0)
    sums[...] = tall.reshape(sums.shape)
    pl.semaphore_wait(barrier, devices - 1)

    def one(k):
        index, device = peer(k)
        return remote(sums.at[index], parts.at[k], s_one.at[k], r_one.at[k], device)

    def two(k):
        return remote(piece, totals.at[me], s_two.at[k], r_two.at[k], peer(k)[1])

    def span(index):
        return pl.ds(pl.multiple_of(index * chunk, chunk), chunk)

    def send(k):
        dest = (here + k) % wide
        return remote(
            packed.at[span(dest)], gath_ref.at[span(here)], s_send.at[k], r_send.at[k], (dest, side)
        )

    def forward(held, k):
        source = (here - k + wide) % wide
        return remote(
            held.at[span(source)], gath_ref.at[span(wide + source)],
            s_pair.at[k], r_pair.at[k], partner,
        )

    def each(low, high, action):
        def body(k, carry):
            action(k)
            return carry

        lax.fori_loop(low, high, body, 0)

    each(1, devices, lambda k: one(k).start())
    parts[0] = sums[me]
    each(1, wide // 2, lambda k: send(k).start())
    keep = pltpu.make_async_copy(packed.at[span(here)], gath_ref.at[span(here)], s_own)
    keep.start()
    forward(packed, 0).start()
    each(1, devices, lambda k: one(k).wait_recv())
    whole = jnp.sum(parts[...], axis=0)
    piece[...] = whole
    totals[me] = whole
    each(1, devices, lambda k: two(k).start())
    each(wide // 2, wide, lambda k: send(k).start())
    each(1, devices, lambda k: two(k).wait_recv())

    tall = totals[...].reshape(devices * totals.shape[1], 128)
    step = tall.shape[0] // (width // 128)
    both = jnp.concatenate([tall[p * step : (p + 1) * step] for p in range(width // 128)], axis=1)

    def spread(folded):
        return jnp.where(mask, jnp.concatenate([folded] * HEADS, axis=0), 0.0).astype(BF16)

    summary, grad_summary = spread(both[:head_dim]), spread(both[head_dim:])

    def back(grad, unit, scale):
        mean_grad = dot_split(grad, mean_mat)
        mean_cross = dot_split(grad * unit, mean_mat)
        return ((grad - mean_grad - unit * mean_cross) / scale).astype(BF16)

    mixed = dot(q, summary).astype(BF16)
    grad_query = dot(grad_mixed, summary, 1, 1).astype(BF16)
    grad_key = back(dot(v_norm, grad_summary, 1, 1), k_unit, k_scale)
    grad_value = back(dot(k_norm, grad_summary), v_unit, v_scale)
    x_turned = x.T
    mixed_turned = mixed.T
    for block, (left, right) in enumerate(
        [(x_turned, grad_query), (x_turned, grad_key), (x_turned, grad_value), (mixed_turned, cot)]
    ):
        value = (dot(left, right) * (1.0 / total)).reshape(wide, narrow, -1, width)
        for part in range(narrow):
            att[part, :, :, block * width : (block + 1) * width] = value[:, part].astype(BF16)
    swap = remote(att.at[1 - side], theirs, s_half, r_half, partner)
    swap.start()
    out_ref[...] = x.astype(F32) + dot(mixed, wout_ref[...])
    back_ref[...] = (
        cot.astype(F32)
        + dot(grad_query, wqkv_ref[:, :width], 1, 1)
        + dot(grad_key, wqkv_ref[:, width : 2 * width], 1, 1)
        + dot(grad_value, wqkv_ref[:, 2 * width :], 1, 1)
    )
    swap.wait()
    mine_ref[...] = (att[side].astype(F32) + theirs[...].astype(F32)).astype(BF16)

    def pass_on(k):
        send(k).wait_recv()
        forward(gath_ref, k).start()

    each(1, wide, pass_on)
    keep.wait()
    forward(packed, 0).wait()
    each(1, wide, lambda k: forward(gath_ref, k).wait())
    each(1, wide, lambda k: send(k).wait_send())
    each(1, devices, lambda k: one(k).wait_send())
    each(1, devices, lambda k: two(k).wait_send())


def split_rows(block, slot_rows):
    rows, width = block.shape
    floats = block.astype(F32).reshape(rows // (2 * slot_rows), 2, slot_rows, width)
    return [floats[:, i].reshape(rows // 2, width).astype(BF16) for i in range(2)]


def region_kernel(
    dims, gath_ref, win_ref, bias_ref, wout_ref, mine_ref,
    hidden_ref, gpre_ref, first_ref, late_ref, gatt_ref,
    feats, cots, out_acc, back_acc, ret_send, ret_recv, stage_one, stage_sum, stage_two,
    s_ret, r_ret, s_one, r_one, s_two, r_two,
):
    wide, plane, experts, block_len = dims
    levels = wide // plane
    early = ret_send.shape[0]
    slot_rows = DOMAIN_REPEAT_CAP * block_len
    chunk = 2 * slot_rows
    here, side = lax.axis_index("wide"), lax.axis_index("narrow")
    level, spot = here // plane, here % plane
    expert, step = pl.program_id(0), pl.program_id(1)
    last_step = pl.num_programs(1) - 1
    own, width = out_acc.shape

    def each(low, high, action):
        def body(k, carry):
            action(k)
            return carry

        lax.fori_loop(low, high, body, 0)

    def span(index):
        return pl.ds(pl.multiple_of(index * chunk, chunk), chunk)

    def give(e, k):
        dest = (here + k) % wide
        return remote(
            ret_send.at[e, span(dest)], ret_recv.at[e, span(here)],
            s_ret.at[e, k], r_ret.at[e, k], (dest, side),
        )

    def one(k):
        other = (spot + k) % plane
        return remote(
            mine_ref.at[:, other], stage_one.at[k], s_one.at[k], r_one.at[k],
            (level * plane + other, side),
        )

    def two(k):
        other = (level + k) % levels
        return remote(
            stage_sum.at[other], stage_two.at[k], s_two.at[k], r_two.at[k],
            (other * plane + spot, side),
        )

    @pl.when((expert == 0) & (step == 0))
    def _():
        barrier = pltpu.get_barrier_semaphore()
        each(
            1, wide,
            lambda k: pl.semaphore_signal(
                barrier, inc=1, device_id=((here + k) % wide, side), device_id_type=MESH
            ),
        )
        pl.semaphore_wait(barrier, wide - 1)
        each(1, plane, lambda k: one(k).start())
        stage_one[0] = mine_ref[:, spot]

    @pl.when((expert == 1) & (step == 0))
    def _():
        each(1, plane, lambda k: one(k).wait())
        summed = jnp.sum(stage_one[...].astype(F32), axis=0).astype(BF16)
        stage_sum[...] = summed
        each(1, levels, lambda k: two(k).start())
        stage_two[0] = stage_sum[level]

    @pl.when(step == 0)
    def _():
        feats[...], cots[...] = split_rows(gath_ref[...], slot_rows)

    w_in, w_out = win_ref[...], wout_ref[...]
    pre = dot(feats[...], w_in) + bias_ref[...]
    grad_hidden = dot(cots[...], w_out, 1, 1)
    square = pre * pre
    tangent = jnp.tanh(gelu_scale * (pre + gelu_cubic * square * pre))
    half_sum = 0.5 * (1.0 + tangent)
    hidden = (pre * half_sum).astype(BF16)
    slope = half_sum + 0.5 * pre * (1.0 - tangent * tangent) * gelu_scale * (1.0 + 3.0 * gelu_cubic * square)
    grad_pre = (grad_hidden * slope).astype(BF16)
    hidden_ref[...] = hidden
    gpre_ref[...] = grad_pre
    out_part = dot(hidden[:own], w_out)
    back_part = dot(grad_pre[:own], w_in, 1, 1)

    @pl.when(step == 0)
    def _():
        out_acc[...] = out_part
        back_acc[...] = back_part

    @pl.when(step > 0)
    def _():
        out_acc[...] += out_part
        back_acc[...] += back_part

    @pl.when(step == last_step)
    def _():
        pair = jnp.concatenate(
            [ref[...].reshape(wide, slot_rows, width) for ref in (out_acc, back_acc)], axis=1
        )
        pair = pair.astype(BF16)

        @pl.when(expert < early)
        def _():
            ret_send[expert] = pair.reshape(wide * chunk, width)
            each(1, wide, lambda k: give(expert, k).start())
            ret_recv[expert, span(here), :] = ret_send[expert, span(here), :]

        @pl.when(expert >= early)
        def _():
            late_ref[:, expert - early] = pair

    @pl.when((expert == experts - 1) & (step == last_step))
    def _():
        each(1, levels, lambda k: two(k).wait())
        gatt_ref[...] = jnp.sum(stage_two[...].astype(F32), axis=0)
        for e in range(early):
            each(1, wide, lambda k: give(e, k).wait())
            first_ref[e] = ret_recv[e]


def sum_kernel(
    block_len, experts, col_ref, row_ref, first_ref, late_ref, out_base_ref, back_base_ref, out_ref, back_ref
):
    early = first_ref.shape[0]
    rows = first_ref.shape[1]
    width = out_ref.shape[1]
    have = slot_have(block_len, col_ref[...], row_ref[...])
    out, back = out_base_ref[...], back_base_ref[...]
    for e in range(experts):
        first, second = slot_picks(block_len, experts, e, rows, have)
        if e < early:
            data = first_ref[e]
        else:
            data = late_ref[:, e - early].reshape(rows, width)
        out += dot(first, data, 0, 0)
        back += dot(second, data, 0, 0)
    out_ref[...] = out.astype(BF16)
    back_ref[...] = back.astype(BF16)


def weight_kernel(
    share, slot_rows, half_ref, gath_feat_ref, hidden_ref, gpre_ref, gin_ref, gout_ref, gbias_ref, feats, cots
):
    @pl.when(pl.program_id(1) == 0)
    def _():
        feat, cot = split_rows(gath_feat_ref[...], slot_rows)
        feats[...] = feat.T
        cots[...] = cot

    grad_pre = gpre_ref[...]
    gin_ref[...] = dot(feats[...], grad_pre) * share
    gout_ref[...] = dot(hidden_ref[...], cots[...], 0, 0) * share
    gbias_ref[...] = jnp.sum(grad_pre.astype(F32), axis=0, keepdims=True) * share


def on_device(
    point_feats, region_ids, w_qkv, w_out, w_expert_in, b_expert_in, w_expert_out, out_cotangent
):
    wide = lax.axis_size("wide")
    narrow = lax.axis_size("narrow")
    devices = wide * narrow
    points, width = point_feats.shape
    total = points * devices
    block_len = points // region_ids.shape[0]
    slab = w_expert_in.shape[1]
    experts = DOMAIN_SPECIALS // wide
    plane = 4
    if narrow != 2 or experts < 2 or wide % plane or width % (16 * devices):
        return on_device_plain(
            point_feats, region_ids, w_qkv, w_out, w_expert_in, b_expert_in, w_expert_out, out_cotangent
        )
    hid = slab // experts
    slot_rows = DOMAIN_REPEAT_CAP * block_len
    chunk = 2 * slot_rows
    fold_rows = 2 * (width // HEADS) * (width // 128) // devices
    share_rows = width // devices
    labels = jnp.repeat(region_ids, block_len)
    col, row = labels[:, None], labels[None, :]
    wide_bf = jax.ShapeDtypeStruct((points, width), BF16)
    wide_f = jax.ShapeDtypeStruct((points, width), F32)
    dma = pltpu.SemaphoreType.DMA

    def remote_params(identity, vmem):
        return pltpu.CompilerParams(
            collective_id=identity, has_side_effects=True, vmem_limit_bytes=vmem * 2**20
        )

    gathered, mine, out_base, back_base = pl.pallas_call(
        functools.partial(attend_kernel, (wide, narrow, experts, block_len, total)),
        out_shape=(
            jax.ShapeDtypeStruct((narrow * wide * chunk, experts * width), BF16),
            jax.ShapeDtypeStruct((wide, share_rows, 4 * width), BF16),
            wide_f, wide_f,
        ),
        in_specs=[VMEM_SPEC] * 2 + [HBM_SPEC] * 4,
        out_specs=[HBM_SPEC] + [VMEM_SPEC] * 3,
        scratch_shapes=[
            pltpu.VMEM(point_feats.shape, BF16),
            pltpu.VMEM(out_cotangent.shape, BF16),
            pltpu.VMEM(w_qkv.shape, BF16),
            pltpu.VMEM(w_out.shape, BF16),
            pltpu.VMEM((wide * chunk, experts * width), BF16),
            pltpu.VMEM((devices, fold_rows, 128), F32),
            pltpu.VMEM((devices, fold_rows, 128), F32),
            pltpu.VMEM((fold_rows, 128), F32),
            pltpu.VMEM((devices, fold_rows, 128), F32),
            pltpu.VMEM((narrow, wide, share_rows, 4 * width), BF16),
            pltpu.VMEM((wide, share_rows, 4 * width), BF16),
            dma((devices,)), dma((devices,)), dma((devices,)), dma((devices,)),
            dma((wide,)), dma((wide,)), dma((wide,)), dma((wide,)), dma, dma, dma((4,)), dma,
        ],
        compiler_params=remote_params(0, 60),
        name="attend",
    )(col, row, point_feats, out_cotangent, w_qkv, w_out)

    own = wide * slot_rows
    all_rows = own * narrow
    tile = min(512, hid)
    steps = hid // tile
    levels = wide // plane
    slab_bf = jax.ShapeDtypeStruct((all_rows, slab), BF16)
    early = experts // 2
    hidden, grad_pre, ret_first, ret_late, grad_attention = pl.pallas_call(
        functools.partial(region_kernel, (wide, plane, experts, block_len)),
        out_shape=(
            slab_bf, slab_bf,
            jax.ShapeDtypeStruct((early, wide * chunk, width), BF16),
            jax.ShapeDtypeStruct((wide, experts - early, chunk, width), BF16),
            jax.ShapeDtypeStruct((share_rows, 4 * width), F32),
        ),
        grid=(experts, steps),
        in_specs=[
            pl.BlockSpec((narrow * wide * chunk, width), lambda e, t: (0, e)),
            pl.BlockSpec((width, tile), lambda e, t: (0, e * steps + t)),
            pl.BlockSpec((1, tile), lambda e, t: (0, e * steps + t)),
            pl.BlockSpec((tile, width), lambda e, t: (e * steps + t, 0)),
        ] + [VMEM_SPEC],
        out_specs=[
            pl.BlockSpec((all_rows, tile), lambda e, t: (0, e * steps + t)),
            pl.BlockSpec((all_rows, tile), lambda e, t: (0, e * steps + t)),
        ] + [VMEM_SPEC] * 3,
        scratch_shapes=[
            pltpu.VMEM((all_rows, width), BF16),
            pltpu.VMEM((all_rows, width), BF16),
            pltpu.VMEM((own, width), F32),
            pltpu.VMEM((own, width), F32),
            pltpu.VMEM((early, wide * chunk, width), BF16),
            pltpu.VMEM((early, wide * chunk, width), BF16),
            pltpu.VMEM((plane, levels, share_rows, 4 * width), BF16),
            pltpu.VMEM((levels, share_rows, 4 * width), BF16),
            pltpu.VMEM((levels, share_rows, 4 * width), BF16),
            dma((early, wide)), dma((early, wide)),
            dma((plane,)), dma((plane,)), dma((levels,)), dma((levels,)),
        ],
        compiler_params=remote_params(1, 56),
        name="regions",
    )(
        gathered, w_expert_in, b_expert_in[None, :], w_expert_out,
        mine.reshape(levels, plane, share_rows, 4 * width),
    )
    late_rows = (experts - early) * chunk
    ret_late = lax.all_to_all(
        ret_late.reshape(wide * late_rows, width), "wide", split_axis=0, concat_axis=0, tiled=True
    ).reshape(wide, experts - early, chunk, width)

    half = width // narrow
    side = lax.axis_index("narrow")
    wtile = min(1024, hid)
    wsteps = hid // wtile
    grad_in, grad_out_w, grad_bias = pl.pallas_call(
        functools.partial(weight_kernel, DOMAIN_SPECIALS / total, slot_rows),
        out_shape=(
            jax.ShapeDtypeStruct((half, slab), F32),
            jax.ShapeDtypeStruct((slab, half), F32),
            jax.ShapeDtypeStruct((1, slab), F32),
        ),
        grid_spec=pltpu.PrefetchScalarGridSpec(
            num_scalar_prefetch=1,
            grid=(experts, wsteps),
            in_specs=[
                pl.BlockSpec((narrow * wide * chunk, half), lambda e, t, n: (0, e * narrow + n[0])),
                pl.BlockSpec((all_rows, wtile), lambda e, t, n: (0, e * wsteps + t)),
                pl.BlockSpec((all_rows, wtile), lambda e, t, n: (0, e * wsteps + t)),
            ],
            out_specs=[
                pl.BlockSpec((half, wtile), lambda e, t, n: (0, e * wsteps + t)),
                pl.BlockSpec((wtile, half), lambda e, t, n: (e * wsteps + t, 0)),
                pl.BlockSpec((1, wtile), lambda e, t, n: (0, e * wsteps + t)),
            ],
            scratch_shapes=[pltpu.VMEM((half, all_rows), BF16), pltpu.VMEM((all_rows, half), BF16)],
        ),
        name="weights",
        **params(8 * all_rows * half * slab, 8 * width * slab, 56),
    )(side.astype(jnp.int32)[None], gathered, hidden, grad_pre)
    layer_out, grad_feats = pl.pallas_call(
        functools.partial(sum_kernel, block_len, experts),
        out_shape=(wide_bf, wide_bf),
        in_specs=[VMEM_SPEC] * 6,
        out_specs=[VMEM_SPEC] * 2,
        name="sum",
        **params(8 * points * all_rows * width, 8 * all_rows * width, 24),
    )(col, row, ret_first, ret_late, out_base, back_base)
    bias_half = slab // narrow
    grad_bias_out = lax.dynamic_slice_in_dim(grad_bias[0], side * bias_half, bias_half, 0)
    return (layer_out, grad_feats, grad_attention, grad_in, grad_out_w, grad_bias_out)


def solution(mesh):
    placed = (
        P(("wide", "narrow"), None),
        P(("wide", "narrow")),
        P(),
        P(),
        P(None, "wide"),
        P("wide"),
        P("wide", None),
        P(("wide", "narrow"), None),
    )
    return jax.shard_map(
        on_device,
        mesh=mesh,
        in_specs=placed,
        out_specs=(
            P(("wide", "narrow"), None),
            P(("wide", "narrow"), None),
            P(("wide", "narrow"), None),
            P("narrow", "wide"),
            P("wide", "narrow"),
            P(("wide", "narrow")),
        ),
        check_vma=False,
    )
```
